32 devices in a mesh: replica: 8 (over y, x, core), tensor: 4 (over z).
Axes of the slice: x: 2, y: 2, z: 4, core: 2. Of those that a mesh axis runs over, the one named last changes fastest.
Arguments:
- attention_output: bfloat16 [4, 128, 16384], P(None, 'replica', 'tensor'), may hold values from -6 to 6
- output_weight: bfloat16 [16384, 16384], P('tensor', 'replica'), may hold values from -0.0625 to 0.0625
- adapter_down_weight: bfloat16 [64, 16384, 64], P('replica', 'tensor'), may hold values from -0.046875 to 0.046875
- adapter_up_weight: bfloat16 [64, 64, 16384], P(None, None, ('replica', 'tensor')), may hold values from -0.75 to 0.75
- request_adapter: int32 [128], replicated, may hold values from 0 to 63, as said below
- adapter_storage_row: int32 [64], replicated, may hold values from 0 to 63, as said below
Outputs:
- mixed: bfloat16 [4, 128, 16384], P(None, None, ('replica', 'tensor'))
The draws below stay inside these ranges and needn't reach their ends.
Inputs may be any that keep to these rules, and one draw needn't show every extreme that they name: `request_adapter`: adapter ids of requests; at most 48 requests use adapters whose storage rows lie on one index of replica (rows q * 8 to (q + 1) * 8 - 1), and one index has exactly 48. `adapter_storage_row`: a permutation: every storage row holds exactly one adapter.
All inputs are finite; a program needn't handle non-finite values.
Results may differ from the reference program's by a relative error of at most 0.0029.
Values may be sent and summed in bfloat16 or wider, within the bound.
No kernel may reach another device: no remote copies, remote signals or barrier semaphores. Data moves between devices by JAX's collectives and lax.ppermute only.
A program may use at most 128 MiB of HBM per device.

```python
import jax
import jax.numpy as jnp
from jax import lax

MODEL_WIDTH = 16384
ADAPTER_RANK = 64
STEPS = 4
REQ_DEV = 16
ADAPT_DEV = 8
ATTENTION_FEATS = 16384
REQS = 128
ADAPTER_COUNT = 64
OWN_CAP = 48


def shared_tables(key):
    storage = jax.random.permutation(jax.random.fold_in(key, 11), ADAPTER_COUNT).astype(jnp.int32)
    owners = REQS // REQ_DEV
    hot_owner = jax.random.randint(jax.random.fold_in(key, 12), (), 0, owners)
    order_perm = jax.random.permutation(jax.random.fold_in(key, 13), REQS).astype(jnp.int32)
    rank_of = jnp.zeros((REQS,), jnp.int32).at[order_perm].set(jnp.arange(REQS, dtype=jnp.int32))
    rest_rank = jnp.maximum(rank_of - OWN_CAP, 0)
    other_owner = (hot_owner + 1 + jnp.mod(rest_rank, owners - 1)) % owners
    owner_of = jnp.where(rank_of < OWN_CAP, hot_owner, other_owner)
    inner_slot = jax.random.randint(jax.random.fold_in(key, 14), (REQS,), 0, ADAPT_DEV)
    slot_req = owner_of * ADAPT_DEV + inner_slot
    adapter_at = jnp.argsort(storage).astype(jnp.int32)
    adapter_ids = adapter_at[slot_req]
    return (storage, adapter_ids.astype(jnp.int32))


def draw_request_adapter(key, part):
    return shared_tables(key)[1]


def draw_adapter_storage_row(key, part):
    return shared_tables(key)[0]


def raised(entries, rng, source, target, parts, factor):
    owner, partner = [(jnp.arange(entries.shape[axis_at]) // (entries.shape[axis_at] // parts)).reshape([-1 if axis == axis_at else 1 for axis in range(entries.ndim)]) for axis_at in (source, target)]
    chosen = jax.random.permutation(rng, parts)[partner]
    strong = (owner == chosen) | (owner == (partner + parts // 2) % parts)
    return jnp.where(strong, factor * entries, entries)


def block_scale(key, extent, cuts, low, largest):
    loudness = 1.0
    for position, parts in cuts:
        steps = jax.random.uniform(jax.random.fold_in(jax.random.fold_in(key, 6), position), (parts,), jnp.float32, low / len(cuts), largest / len(cuts))
        loudness = loudness * jnp.repeat(jnp.exp(steps), extent[position] // parts).reshape((-1,) + (1,) * (len(extent) - 1 - position))
    return loudness


def noise(own_key, dims, spread, most, shards=(), held_as=jnp.bfloat16):
    drawn = jax.random.normal(own_key, dims, jnp.float32) * spread
    if len(shards) > 0:
        drawn = block_scale(own_key, dims, shards, -0.22, 0.18) * drawn
    return jnp.clip(drawn, min=-most, max=most).astype(held_as)


def noise_with(own_key, extent, deviation, limit, pieces, heavy, kind=jnp.bfloat16):
    array = deviation * jax.random.normal(own_key, extent, jnp.float32)
    if pieces:
        array = array * block_scale(own_key, extent, pieces, -0.22, 0.18)
    return jnp.clip(raised(array, jax.random.fold_in(own_key, 3), *heavy), -limit, limit).astype(kind)


def setup_inputs(seed: int = 0) -> dict:
    splits = jax.random.split(jax.random.key(seed), 7)
    attention_output = noise(splits[0], (STEPS, REQS, ATTENTION_FEATS), 1.0, 6.0, ((1, 8), (2, 4)))
    output_weight = noise_with(splits[1], (ATTENTION_FEATS, MODEL_WIDTH), ATTENTION_FEATS ** -0.5, 0.0625, ((0, 4), (1, 8)), (0, 1, 8, 2.0))
    adapter_down_weight = noise(splits[2], (ADAPTER_COUNT, ATTENTION_FEATS, ADAPTER_RANK), ATTENTION_FEATS ** -0.5, 0.046875, ((0, 8), (1, 4)))
    adapter_up_weight = noise(splits[3], (ADAPTER_COUNT, ADAPTER_RANK, MODEL_WIDTH), ADAPTER_RANK ** -0.5, 0.75, ((2, 32),))
    request_adapter = draw_request_adapter(jax.random.fold_in(splits[6], 71), 0)
    adapter_storage_row = draw_adapter_storage_row(jax.random.fold_in(splits[6], 71), 0)
    return dict(attention_output=attention_output, output_weight=output_weight, adapter_down_weight=adapter_down_weight, adapter_up_weight=adapter_up_weight, request_adapter=request_adapter, adapter_storage_row=adapter_storage_row)


adapter_scale = 0.5


def reference(attention_output, output_weight, adapter_down_weight, adapter_up_weight, request_adapter, adapter_storage_row):
    storage_row_of = adapter_storage_row[request_adapter].astype(jnp.int32)
    flat_rows = attention_output.reshape(STEPS * REQS, ATTENTION_FEATS)
    base_output = jnp.dot(flat_rows, output_weight, preferred_element_type=jnp.float32).reshape(STEPS, REQS, MODEL_WIDTH)
    rows_per_request = jnp.transpose(attention_output, (1, 0, 2))

    def request_partial(packed):
        row_block, storage_index = packed
        down_output = lax.dynamic_index_in_dim(adapter_down_weight, storage_index.astype(jnp.int32), 0, keepdims=False)
        up_output = lax.dynamic_index_in_dim(adapter_up_weight, storage_index.astype(jnp.int32), 0, keepdims=False)
        rank_full = jnp.dot(row_block, down_output, preferred_element_type=jnp.float32)
        rank_values = rank_full.astype(jnp.bfloat16)
        return jnp.dot(rank_values, up_output, preferred_element_type=jnp.float32)

    adapter_delta = lax.map(request_partial, (rows_per_request, storage_row_of))
    adapter_delta = jnp.transpose(adapter_delta, (1, 0, 2))
    return (base_output + adapter_scale * adapter_delta).astype(jnp.bfloat16)
```

```python
import functools

import jax
import jax.numpy as jnp
from jax import lax
from jax.experimental import pallas as pl
from jax.experimental.pallas import tpu as pltpu
from jax.sharding import PartitionSpec as P

OWN_CAP = 48


adapter_scale = 0.5

MIB = 2**20
VMEM = pl.BlockSpec(memory_space=pltpu.VMEM)


def params(mib):
    return pltpu.CompilerParams(vmem_limit_bytes=mib * MIB)


def stack_rows(parts, rows_ref):
    at = 0
    for part in parts:
        steps, requests, feats = part.shape
        rows_ref[pl.ds(at, steps * requests), :] = part[...].reshape(steps * requests, feats)
        at += steps * requests


def column_dot(rows_ref, weight_ref, chunk, store, cols, width):
    for at in range(0, cols, width):
        off = pl.multiple_of(chunk * cols + at, width)
        store(
            pl.ds(at, width),
            jnp.dot(rows_ref[...], weight_ref[:, pl.ds(off, width)], preferred_element_type=jnp.float32),
        )


def base_out_kernel(n, *refs):
    parts, weight, near, rows = refs[:n], refs[n], refs[n + 1], refs[n + 2]
    cols = near.shape[-1]
    mine = lax.axis_index("tensor")
    stack_rows(parts, rows)
    for slot, flip in enumerate((1, 3)):

        def store(where, value, slot=slot):
            near[slot, :, where] = value.astype(near.dtype)

        column_dot(rows, weight, mine ^ flip, store, cols, 256)


def base_in_kernel(n, *refs):
    parts, weight, far, own, rows = refs[:n], refs[n], refs[n + 1], refs[n + 2], refs[n + 3]
    cols = own.shape[-1]
    mine = lax.axis_index("tensor")
    stack_rows(parts, rows)
    for flip, out in ((2, far), (0, own)):

        def store(where, value, out=out):
            out[:, where] = value

        column_dot(rows, weight, mine ^ flip, store, cols, 256)


def rank_kernel(order, n, *refs):
    parts, down, slot, place = refs[:n], refs[n], refs[n + 1], refs[n + 2]
    out, rows = refs[n + 3], refs[n + 4]
    me = lax.axis_index("replica")
    adapters, rank = down.shape[0], down.shape[1]
    feats = down.shape[2]
    steps = 4
    for (k, first), part in zip(order, parts):
        count = part.shape[0] * part.shape[1]
        whole = steps * part.shape[1]
        at = pl.multiple_of((me ^ k) * whole + first * part.shape[1], part.shape[1])
        rows[pl.ds(at, count), :] = part[...].reshape(count, feats)
    total = rows.shape[0]
    reduced = lax.dot_general(
        rows[...],
        down[...].reshape(adapters * rank, feats),
        (((1,), (1,)), ((), ())),
        preferred_element_type=jnp.float32,
    )
    local = slot[...] - me * adapters
    adapter_of = lax.broadcasted_iota(jnp.int32, (total, adapters * rank), 1) // rank
    picked = jnp.where(adapter_of == local, reduced, 0.0)
    width = adapters * rank
    while width > rank:
        width //= 2
        picked = picked[:, :width] + picked[:, width:]
    packed = steps * OWN_CAP
    where = place[...] - me * packed
    chosen = (lax.broadcasted_iota(jnp.int32, (packed, total), 0) == where).astype(jnp.float32)
    packed_rank = jnp.dot(
        chosen, picked, preferred_element_type=jnp.float32, precision=lax.Precision.HIGHEST
    )
    half = packed // 2
    out[...] = jnp.concatenate([packed_rank[:half], packed_rank[half:]], axis=1)


def up_kernel(packed_rank, up, slot, column, out):
    total = slot.shape[0]
    adapters, rank, cols = up.shape
    owners, held, _ = packed_rank.shape
    chosen = (
        lax.broadcasted_iota(jnp.int32, (total, owners * held), 1) == column[...]
    ).astype(jnp.bfloat16)
    both = jnp.dot(
        chosen, packed_rank[...].reshape(owners * held, 2 * rank), preferred_element_type=jnp.float32
    )
    late = (lax.broadcasted_iota(jnp.int32, (total, rank), 0) // 32) % 2
    rank_rows = jnp.where(late == 1, both[:, rank:], both[:, :rank])
    group = 8
    wide = jnp.concatenate([rank_rows] * group, axis=1).astype(jnp.bfloat16)
    adapter_of = lax.broadcasted_iota(jnp.int32, (total, group * rank), 1) // rank
    local = slot[...] - adapter_of
    out[...] = jnp.zeros_like(out)

    def step(g, carry):
        spread = jnp.where(local == g * group, wide, jnp.zeros_like(wide))
        weight = up[pl.ds(g * group, group)].reshape(group * rank, cols)
        out[...] += jnp.dot(spread, weight, preferred_element_type=jnp.float32)
        return carry

    lax.fori_loop(0, adapters // group, step, 0)
    out[...] = adapter_scale * out[...]


def finish_kernel(pieces, *refs):
    out, delta = refs[-1], refs[-2]
    steps, _, cols = out.shape
    me = lax.axis_index("replica")
    at = 0
    for order in pieces:
        own, near, far, mid = refs[at : at + 4]
        at += 4
        rows = own.shape[0] // len(order)
        requests = rows // steps
        for i, k in enumerate(order):
            here = pl.ds(i * rows, rows)
            who = me ^ k
            total = own[here, :] + near[0, here, :].astype(jnp.float32)
            total += far[here, :].astype(jnp.float32) + mid[here, :].astype(jnp.float32)
            total += delta[pl.ds(pl.multiple_of(who * rows, rows), rows), :]
            out[:, pl.ds(pl.multiple_of(who * requests, requests), requests), :] = total.astype(
                out.dtype
            ).reshape(steps, requests, cols)


def flip(size, bits):
    return [(i, i ^ bits) for i in range(size)]


def on_device_blocks(
    attention_output,
    output_weight,
    adapter_down_weight,
    adapter_up_weight,
    request_adapter,
    adapter_storage_row,
):
    replicas = lax.axis_size("replica")
    steps, own_requests, feats = attention_output.shape
    tensors = lax.axis_size("tensor")
    cols = output_weight.shape[1] // tensors
    adapters_here = adapter_down_weight.shape[0]
    requests = request_adapter.shape[0]
    mine = lax.axis_index("tensor")
    inner = (mine == 1) | (mine == 2)

    def swap(value, bits):
        return lax.ppermute(value, "replica", flip(replicas, bits))

    half = steps // 2
    x0 = attention_output
    x1 = swap(x0, 1)
    x2 = swap(x0, 2)
    x4 = swap(x0, 4)
    x3 = swap(x2, 1)
    x5 = swap(x4, 1)
    x6a = swap(x2[:half], 4)
    x6b = swap(x4[half:], 2)
    x7a = swap(x6a, 1)
    x7b = swap(x6b, 1)

    adapter_ids = jnp.arange(adapter_storage_row.shape[0], dtype=jnp.int32)
    slot_of = jnp.sum(
        jnp.where(request_adapter[:, None] == adapter_ids[None, :], adapter_storage_row[None, :], 0),
        axis=1,
    )
    owner_of = slot_of // adapters_here
    index = jnp.arange(requests, dtype=jnp.int32)
    rank_in = jnp.sum(
        ((owner_of[:, None] == owner_of[None, :]) & (index[None, :] < index[:, None])).astype(jnp.int32),
        axis=1,
    )

    def by_row(per_request, per_step):
        grid = per_request.reshape(replicas, 1, own_requests) + per_step.reshape(1, steps, 1)
        return grid.reshape(replicas * steps * own_requests)

    step = jnp.arange(steps, dtype=jnp.int32)
    slot_rows = by_row(slot_of, 0 * step)[:, None]
    place_rows = by_row(owner_of * (steps * OWN_CAP) + rank_in, step * OWN_CAP)[None, :]
    column_rows = by_row(owner_of * (half * OWN_CAP) + rank_in, (step % half) * OWN_CAP)[:, None]

    def base(parts):
        rows = sum(p.shape[0] * p.shape[1] for p in parts)
        n = len(parts)
        scratch = [pltpu.VMEM((rows, feats), jnp.bfloat16)]
        cost = pl.CostEstimate(flops=4 * rows * feats * cols, bytes_accessed=4 * rows * feats, transcendentals=0)
        near = pl.pallas_call(
            functools.partial(base_out_kernel, n),
            out_shape=jax.ShapeDtypeStruct((2, rows, cols), jnp.bfloat16),
            in_specs=[VMEM] * (n + 1),
            out_specs=VMEM,
            scratch_shapes=scratch,
            compiler_params=params(16),
            cost_estimate=cost,
        )(*parts, output_weight)
        near_in = lax.ppermute(near, "tensor", flip(tensors, 1))
        mid_in = lax.ppermute(near[1], "tensor", [(1, 2), (2, 1)])
        far, own = pl.pallas_call(
            functools.partial(base_in_kernel, n),
            out_shape=[jax.ShapeDtypeStruct((rows, cols), jnp.float32)] * 2,
            in_specs=[VMEM] * (n + 1),
            out_specs=[VMEM, VMEM],
            scratch_shapes=scratch,
            compiler_params=params(16),
            cost_estimate=cost,
        )(*parts, output_weight)
        passed = (far + jnp.where(inner, near_in[1].astype(jnp.float32), 0.0)).astype(jnp.bfloat16)
        far_in = lax.ppermute(passed, "tensor", flip(tensors, 2))
        return own, near_in, far_in, mid_in

    first = base([x0, x1])
    second = base([x2, x3, x4, x5])

    order = [(0, 0), (1, 0), (2, 0), (3, 0), (4, 0), (5, 0), (6, 0), (6, half), (7, 0), (7, half)]
    parts = [x0, x1, x2, x3, x4, x5, x6a, x6b, x7a, x7b]
    total_rows = replicas * steps * own_requests
    down = jnp.transpose(adapter_down_weight, (0, 2, 1))
    rank = down.shape[1]
    packed = pl.pallas_call(
        functools.partial(rank_kernel, order, len(parts)),
        out_shape=jax.ShapeDtypeStruct((half * OWN_CAP, 2 * rank), jnp.float32),
        in_specs=[VMEM] * (len(parts) + 3),
        out_specs=VMEM,
        scratch_shapes=[pltpu.VMEM((total_rows, feats), jnp.bfloat16)],
        compiler_params=params(20),
        cost_estimate=pl.CostEstimate(
            flops=2 * total_rows * feats * adapters_here * rank, bytes_accessed=4 * MIB, transcendentals=0
        ),
    )(*parts, down, slot_rows, place_rows)
    gathered = packed
    for bits in (1, 2, 3):
        gathered = gathered + lax.ppermute(packed, "tensor", flip(tensors, bits))
    third = base([x6a, x6b, x7a, x7b])
    ranks = lax.all_gather(gathered.astype(jnp.bfloat16), "replica", axis=0)
    delta = pl.pallas_call(
        up_kernel,
        out_shape=jax.ShapeDtypeStruct((total_rows, cols), jnp.float32),
        in_specs=[VMEM] * 4,
        out_specs=VMEM,
        compiler_params=params(20),
        cost_estimate=pl.CostEstimate(
            flops=2 * total_rows * cols * adapter_up_weight.shape[0] * rank,
            bytes_accessed=4 * MIB,
            transcendentals=0,
        ),
    )(ranks, adapter_up_weight, slot_rows, column_rows)

    pieces = [(0, 1), (2, 3, 4, 5), (6, 7)]
    return pl.pallas_call(
        functools.partial(finish_kernel, pieces),
        out_shape=jax.ShapeDtypeStruct((steps, requests, cols), jnp.bfloat16),
        in_specs=[VMEM] * 13,
        out_specs=VMEM,
        compiler_params=params(16),
    )(*first, *second, *third, delta)


def on_device(
    attention_output,
    output_weight,
    adapter_down_weight,
    adapter_up_weight,
    request_adapter,
    adapter_storage_row,
):
    replicas = lax.axis_size("replica")
    my_index = lax.axis_index("replica")
    owner_partial = adapter_down_weight.shape[0]
    requests = request_adapter.shape[0]
    everyone = lax.all_gather(attention_output, "replica", axis=1, tiled=True)
    partial_sums = jnp.einsum(
        "sif,fc->sic", everyone, output_weight, preferred_element_type=jnp.float32
    )
    base_output = lax.psum_scatter(partial_sums, "tensor", scatter_dimension=2, tiled=True)
    adapter_ids = jnp.arange(adapter_storage_row.shape[0], dtype=jnp.int32)
    storage_row_of = jnp.sum(
        jnp.where(
            request_adapter[:, None] == adapter_ids[None, :], adapter_storage_row[None, :], 0
        ),
        axis=1,
    )
    owner_of = storage_row_of // owner_partial
    owner_table = owner_of[:, None] == jnp.arange(replicas, dtype=jnp.int32)[None, :]
    running = jnp.cumsum(owner_table.astype(jnp.int32), axis=0) - 1
    rank_in = jnp.sum(jnp.where(owner_table, running, 0), axis=1)
    owned_here = owner_of == my_index
    target = jnp.where(owned_here, rank_in, OWN_CAP)
    chosen = (
        jnp.zeros((OWN_CAP,), jnp.int32)
        .at[target]
        .set(jnp.arange(requests, dtype=jnp.int32), mode="drop")
    )
    filled = jnp.zeros((OWN_CAP,), jnp.int32).at[target].set(1, mode="drop")
    local_slot = storage_row_of[chosen] - my_index * owner_partial
    slot_pick = jnp.where(
        local_slot[:, None] == jnp.arange(owner_partial, dtype=jnp.int32)[None, :],
        filled[:, None],
        0,
    ).astype(jnp.float32)
    selected_rows = everyone[:, chosen, :]
    reduced_input = jnp.einsum(
        "ldu,hun->ldhn", selected_rows, adapter_down_weight, preferred_element_type=jnp.float32
    )
    rank_part = jnp.sum(reduced_input * slot_pick[None, :, :, None], axis=2)
    spread = jnp.where(
        owned_here[None, :, None], rank_part[:, jnp.minimum(rank_in, OWN_CAP - 1), :], 0.0
    )
    rank_full = lax.psum(spread, ("replica", "tensor"))
    rank_values = rank_full.astype(jnp.bfloat16)
    selected_up_rows = adapter_up_weight[storage_row_of]
    adapter_delta = jnp.einsum(
        "ajz,jzt->ajt", rank_values, selected_up_rows, preferred_element_type=jnp.float32
    )
    return (base_output + adapter_scale * adapter_delta).astype(jnp.bfloat16)


def solution(mesh):
    in_specs = (
        P(None, "replica", "tensor"),
        P("tensor", "replica"),
        P("replica", "tensor", None),
        P(None, None, ("replica", "tensor")),
        P(),
        P(),
    )
    out_specs = P(None, None, ("replica", "tensor"))
    blocks = mesh.shape["replica"] == 8 and mesh.shape["tensor"] == 4
    return jax.shard_map(
        on_device_blocks if blocks else on_device,
        mesh=mesh,
        in_specs=in_specs,
        out_specs=out_specs,
        check_vma=False,
    )
```

```python
import functools

import jax
import jax.numpy as jnp
from jax import lax
from jax.experimental import pallas as pl
from jax.experimental.pallas import tpu as pltpu
from jax.sharding import PartitionSpec as P

OWN_CAP = 48


adapter_scale = 0.5

MIB = 2**20
WIDE = 256
VMEM = pl.BlockSpec(memory_space=pltpu.VMEM)
HBM = pl.BlockSpec(memory_space=pltpu.HBM)


def params(mib):
    return pltpu.CompilerParams(vmem_limit_bytes=mib * MIB)


def stack_rows(parts, rows_ref):
    at = 0
    for part in parts:
        steps, requests, feats = part.shape
        rows_ref[pl.ds(at, steps * requests), :] = part[...].reshape(steps * requests, feats)
        at += steps * requests


def load_kernel(weight, out, sems):
    cols = out.shape[-1]
    mine = lax.axis_index("tensor")
    copies = [
        pltpu.make_async_copy(
            weight.at[:, pl.ds(pl.multiple_of((mine ^ flip) * cols, cols), cols)], out.at[slot], sems.at[slot]
        )
        for slot, flip in enumerate((1, 3))
    ]
    for copy in copies:
        copy.start()
    for copy in copies:
        copy.wait()


def outer_dots(rows, weight, near, mid):
    cols = mid.shape[-1]
    for at in range(0, cols, WIDE):
        where = pl.ds(at, WIDE)
        near[0, :, where] = jnp.dot(
            rows[...], weight[0, :, where], preferred_element_type=jnp.float32
        ).astype(near.dtype)
    for at in range(0, cols, WIDE):
        where = pl.ds(at, WIDE)
        value = jnp.dot(
            rows[...], weight[1, :, where], preferred_element_type=jnp.float32
        ).astype(near.dtype)
        near[1, :, where] = value
        mid[:, where] = value


def first_outer_kernel(n, *refs):
    parts, weight, whole, near, mid, rest, rows, sems = refs[:n], *refs[n:]
    cols = mid.shape[-1]
    mine = lax.axis_index("tensor")
    copies = [
        pltpu.make_async_copy(
            whole.at[:, pl.ds(pl.multiple_of((mine ^ flip) * cols, cols), cols)], rest.at[slot], sems.at[slot]
        )
        for slot, flip in enumerate((2, 0))
    ]
    for copy in copies:
        copy.start()
    stack_rows(parts, rows)
    outer_dots(rows, weight, near, mid)
    for copy in copies:
        copy.wait()


def outer_kernel(n, *refs):
    parts, weight, near, mid, rows = refs[:n], *refs[n:]
    stack_rows(parts, rows)
    outer_dots(rows, weight, near, mid)


def inner_kernel(n, *refs):
    parts, weight, far, own, rows = refs[:n], *refs[n:]
    cols = own.shape[-1]
    stack_rows(parts, rows)
    for slot, out in enumerate((far, own)):
        for at in range(0, cols, WIDE):
            where = pl.ds(at, WIDE)
            out[:, where] = jnp.dot(rows[...], weight[slot, :, where], preferred_element_type=jnp.float32)


def rank_kernel(order, before, n, *refs):
    parts, rest, rows = refs[:n], refs[n:-1], refs[-1]
    down, slot, place, out = rest[0], rest[1], rest[2], rest[-1]
    me = lax.axis_index("replica")
    adapters, rank, feats = down.shape
    stack_rows(parts, rows)
    total = rows.shape[0]
    block = total // len(order)
    starts = [pl.multiple_of((me ^ k) * block, block) for k in order]
    reduced = lax.dot_general(
        rows[...],
        down[...].reshape(adapters * rank, feats),
        (((1,), (1,)), ((), ())),
        preferred_element_type=jnp.float32,
    )
    local = jnp.concatenate([slot[pl.ds(at, block), :] for at in starts], axis=0) - me * adapters
    adapter_of = lax.broadcasted_iota(jnp.int32, (total, adapters * rank), 1) // rank
    picked = jnp.where(adapter_of == local, reduced, 0.0)
    width = adapters * rank
    while width > rank:
        width //= 2
        picked = picked[:, :width] + picked[:, width:]
    half = out.shape[0]
    packed = 2 * half
    where = jnp.concatenate([place[pl.ds(me ^ k, 1), :] for k in order], axis=1) - me * packed
    chosen = (lax.broadcasted_iota(jnp.int32, (packed, total), 0) == where).astype(jnp.float32)
    packed_rank = jnp.dot(
        chosen, picked, preferred_element_type=jnp.float32, precision=lax.Precision.HIGHEST
    )
    value = jnp.concatenate([packed_rank[:half], packed_rank[half:]], axis=1)
    out[...] = value + rest[3][...] if before else value


def up_kernel(packed_rank, up, slot, column, out):
    total = slot.shape[0]
    adapters, rank, cols = up.shape
    owners, held, _ = packed_rank.shape
    chosen = (
        lax.broadcasted_iota(jnp.int32, (total, owners * held), 1) == column[...]
    ).astype(jnp.bfloat16)
    both = jnp.dot(
        chosen, packed_rank[...].reshape(owners * held, 2 * rank), preferred_element_type=jnp.float32
    )
    early_rows = total // owners // 2
    late = (lax.broadcasted_iota(jnp.int32, (total, rank), 0) // early_rows) % 2
    rank_rows = jnp.where(late == 1, both[:, rank:], both[:, :rank])
    group = 8
    wide = jnp.concatenate([rank_rows] * group, axis=1).astype(jnp.bfloat16)
    adapter_of = lax.broadcasted_iota(jnp.int32, (total, group * rank), 1) // rank
    local = slot[...] - adapter_of
    out[...] = jnp.zeros_like(out)

    def step(g, carry):
        spread = jnp.where(local == g * group, wide, jnp.zeros_like(wide))
        weight = up[pl.ds(g * group, group)].reshape(group * rank, cols)
        out[...] += jnp.dot(spread, weight, preferred_element_type=jnp.float32)
        return carry

    lax.fori_loop(0, adapters // group, step, 0)
    out[...] = adapter_scale * out[...]


def finish_kernel(pieces, *refs):
    out, delta = refs[-1], refs[-2]
    steps, _, cols = out.shape
    me = lax.axis_index("replica")
    at = 0
    for order in pieces:
        own, near, far, mid = refs[at : at + 4]
        at += 4
        rows = own.shape[0] // len(order)
        requests = rows // steps
        for i, k in enumerate(order):
            here = pl.ds(i * rows, rows)
            who = me ^ k
            total = own[here, :] + near[0, here, :].astype(jnp.float32)
            total += far[here, :].astype(jnp.float32) + mid[here, :].astype(jnp.float32)
            total += delta[pl.ds(pl.multiple_of(who * rows, rows), rows), :]
            out[:, pl.ds(pl.multiple_of(who * requests, requests), requests), :] = total.astype(
                out.dtype
            ).reshape(steps, requests, cols)


def flip(size, bits):
    return [(i, i ^ bits) for i in range(size)]


def on_device_blocks(
    attention_output,
    output_weight,
    adapter_down_weight,
    adapter_up_weight,
    request_adapter,
    adapter_storage_row,
):
    replicas, tensors = lax.axis_size("replica"), lax.axis_size("tensor")
    steps, own_requests, feats = attention_output.shape
    cols = output_weight.shape[1] // tensors
    adapters_here, _, rank = adapter_down_weight.shape
    requests = request_adapter.shape[0]
    rows = steps * own_requests
    half = steps // 2
    me, mine = lax.axis_index("replica"), lax.axis_index("tensor")
    inner = (mine == 1) | (mine == 2)

    def swap(value, bits):
        return lax.ppermute(value, "replica", flip(replicas, bits))

    def along(value, bits):
        return lax.ppermute(value, "tensor", flip(tensors, bits))

    passed = []

    def tie(*values):
        held = lax.optimization_barrier((*values, *passed))[: len(values)]
        return held[0] if len(values) == 1 else held

    def done(*values):
        passed[:] = values

    def wait(*values):
        passed.extend(values)

    adapter_ids = jnp.arange(adapter_storage_row.shape[0], dtype=jnp.int32)
    slot_of = jnp.sum(
        jnp.where(request_adapter[:, None] == adapter_ids[None, :], adapter_storage_row[None, :], 0),
        axis=1,
    )
    owner_of = slot_of // adapters_here
    index = jnp.arange(requests, dtype=jnp.int32)
    rank_in = jnp.sum(
        ((owner_of[:, None] == owner_of[None, :]) & (index[None, :] < index[:, None])).astype(jnp.int32),
        axis=1,
    )

    def by_row(per_request, per_step):
        return per_request.reshape(replicas, 1, own_requests) + per_step.reshape(1, steps, 1)

    step = jnp.arange(steps, dtype=jnp.int32)
    slot_rows = by_row(slot_of, 0 * step).reshape(-1, 1)
    place_rows = by_row(owner_of * (steps * OWN_CAP) + rank_in, step * OWN_CAP).reshape(replicas, rows)
    column_rows = by_row(
        (owner_of ^ me) * (half * OWN_CAP) + rank_in, (step % half) * OWN_CAP
    ).reshape(-1, 1)

    def cost(n, width):
        return pl.CostEstimate(flops=n * width, bytes_accessed=n, transcendentals=0)

    def outer(parts, *weights):
        n = sum(p.shape[0] * p.shape[1] for p in parts)
        first = len(weights) == 2
        shapes = [
            jax.ShapeDtypeStruct((2, n, cols), jnp.bfloat16),
            jax.ShapeDtypeStruct((n, cols), jnp.bfloat16),
        ]
        scratch = [pltpu.VMEM((n, feats), jnp.bfloat16)]
        return pl.pallas_call(
            functools.partial(first_outer_kernel if first else outer_kernel, len(parts)),
            out_shape=shapes + [pltpu.VMEM((2, feats, cols), jnp.bfloat16)] * first,
            in_specs=[VMEM] * (len(parts) + 1) + [HBM] * first,
            out_specs=[VMEM] * (2 + first),
            scratch_shapes=scratch + [pltpu.SemaphoreType.DMA((2,))] * first,
            compiler_params=params(8),
            cost_estimate=cost(n, 2 * cols),
        )(*parts, *weights)

    def inside(parts, weight):
        n = sum(p.shape[0] * p.shape[1] for p in parts)
        return pl.pallas_call(
            functools.partial(inner_kernel, len(parts)),
            out_shape=[jax.ShapeDtypeStruct((n, cols), jnp.float32)] * 2,
            in_specs=[VMEM] * (len(parts) + 1),
            out_specs=[VMEM, VMEM],
            scratch_shapes=[pltpu.VMEM((n, feats), jnp.bfloat16)],
            compiler_params=params(8),
            cost_estimate=cost(n, 2 * cols),
        )(*parts, weight)

    down = jnp.transpose(adapter_down_weight, (0, 2, 1))

    def ranked(order, parts, *before):
        n = rows * len(order)
        return pl.pallas_call(
            functools.partial(rank_kernel, order, len(before) > 0, len(parts)),
            out_shape=jax.ShapeDtypeStruct((half * OWN_CAP, 2 * rank), jnp.float32),
            in_specs=[VMEM] * (len(parts) + 3 + len(before)),
            out_specs=VMEM,
            scratch_shapes=[pltpu.VMEM((n, feats), jnp.bfloat16)],
            compiler_params=params(10),
            cost_estimate=cost(n, adapters_here * rank),
        )(*parts, down, slot_rows, place_rows, *before)

    def pass_on(far, near_in):
        both = far + jnp.where(inner, near_in[1].astype(jnp.float32), 0.0)
        both = both.astype(jnp.bfloat16)
        return along(both, 2), both

    def across(mid):
        return lax.ppermute(mid, "tensor", [(1, 2), (2, 1)])

    x0 = attention_output
    x1, x2, x4 = swap(x0, 1), swap(x0, 2), swap(x0, 4)
    weight = pltpu.with_memory_space_constraint(output_weight, pltpu.HBM)
    held_out = pl.pallas_call(
        load_kernel,
        out_shape=pltpu.VMEM((2, feats, cols), jnp.bfloat16),
        in_specs=[HBM],
        out_specs=VMEM,
        scratch_shapes=[pltpu.SemaphoreType.DMA((2,))],
        compiler_params=params(2),
    )(weight)
    near0, mid0, held_in = outer([x0, x1], held_out, weight)
    done(near0)
    near0_in, mid0_in = along(near0, 1), across(mid0)
    far0, own0 = inside([tie(x0), x1], held_in)
    done(own0)
    packed = ranked((0, 1), [tie(x0), x1])
    done(packed)

    far0_in, sent = pass_on(far0, tie(near0_in))
    wait(sent)

    wait(x2, x4, mid0_in)
    x2, x4 = tie(x2, x4)
    x3, x6a = swap(x2, 1), swap(x2[:half], 4)
    x5, x6b = swap(x4, 1), swap(x4[half:], 2)
    wait(x3)
    near1, mid1 = outer([tie(x2), x3], held_out)
    done(near1)
    near1_in = along(near1, 1)
    wait(x5)
    mid1_in = across(tie(mid1))
    far1, own1 = inside([tie(x2), x3], held_in)
    done(own1)
    packed = ranked((2, 3), [tie(x2), x3], packed)
    done(packed)

    wait(x6a, x6b)
    x6a, x6b = tie(x6a, x6b)
    x7a, x7b = swap(x6a, 1), swap(x6b, 1)
    near2, mid2 = outer([tie(x4), x5], held_out)
    done(near2)
    wait(x7a, x7b, far0_in)
    near2_in, mid2_in = along(tie(near2), 1), across(tie(mid2))
    packed = ranked((4, 5, 6, 7), [tie(x4), x5, x6a, x6b, x7a, x7b], packed)
    done(packed)
    packed_in = along(packed, 1)
    wait(near1_in, mid1_in)
    far1_in, sent = pass_on(far1, tie(near1_in))
    wait(sent)
    near3, mid3 = outer([tie(x6a), x6b, x7a, x7b], held_out)
    done(near3)
    near3_in = along(near3, 1)
    wait(packed_in)
    packed = packed + tie(packed_in)
    done(packed)
    packed_in = along(packed, 2)
    far2, own2 = inside([tie(x4), x5], held_in)
    done(own2)
    wait(mid2_in, near2_in)
    mid3_in = across(tie(mid3))
    far2_in, sent = pass_on(far2, tie(near2_in))
    wait(sent)
    far3, own3 = inside([tie(x6a), x6b, x7a, x7b], held_in)
    done(own3)
    wait(packed_in)
    ranks = (packed + tie(packed_in)).astype(jnp.bfloat16)[None]
    done(ranks)
    got = swap(ranks, 1)
    wait(far1_in, got)
    ranks = jnp.concatenate([ranks, tie(got)], axis=0)
    done(ranks)
    got = swap(ranks, 2)
    wait(near3_in)
    far3_in, sent = pass_on(far3, tie(near3_in))
    wait(sent, got, far2_in)
    ranks = jnp.concatenate([ranks, tie(got)], axis=0)
    done(ranks)
    got = swap(ranks, 4)
    wait(got, mid3_in)
    ranks = jnp.concatenate([ranks, tie(got)], axis=0)

    delta = pl.pallas_call(
        up_kernel,
        out_shape=jax.ShapeDtypeStruct((replicas * rows, cols), jnp.float32),
        in_specs=[VMEM] * 4,
        out_specs=VMEM,
        compiler_params=params(12),
        cost_estimate=pl.CostEstimate(
            flops=2 * replicas * rows * cols * adapter_up_weight.shape[0] * rank,
            bytes_accessed=4 * MIB,
            transcendentals=0,
        ),
    )(ranks, adapter_up_weight, slot_rows, column_rows)

    pieces = [(0, 1), (2, 3), (4, 5), (6, 7)]
    shares = [
        (own0, near0_in, far0_in, mid0_in),
        (own1, near1_in, far1_in, mid1_in),
        (own2, near2_in, far2_in, mid2_in),
        (own3, near3_in, far3_in, mid3_in),
    ]
    return pl.pallas_call(
        functools.partial(finish_kernel, pieces),
        out_shape=jax.ShapeDtypeStruct((steps, requests, cols), jnp.bfloat16),
        in_specs=[VMEM] * 17,
        out_specs=VMEM,
        compiler_params=params(12),
    )(*[ref for share in shares for ref in share], delta)


def on_device(
    attention_output,
    output_weight,
    adapter_down_weight,
    adapter_up_weight,
    request_adapter,
    adapter_storage_row,
):
    replicas = lax.axis_size("replica")
    my_index = lax.axis_index("replica")
    owner_partial = adapter_down_weight.shape[0]
    requests = request_adapter.shape[0]
    everyone = lax.all_gather(attention_output, "replica", axis=1, tiled=True)
    partial_sums = jnp.einsum(
        "sif,fc->sic", everyone, output_weight, preferred_element_type=jnp.float32
    )
    base_output = lax.psum_scatter(partial_sums, "tensor", scatter_dimension=2, tiled=True)
    adapter_ids = jnp.arange(adapter_storage_row.shape[0], dtype=jnp.int32)
    storage_row_of = jnp.sum(
        jnp.where(
            request_adapter[:, None] == adapter_ids[None, :], adapter_storage_row[None, :], 0
        ),
        axis=1,
    )
    owner_of = storage_row_of // owner_partial
    owner_table = owner_of[:, None] == jnp.arange(replicas, dtype=jnp.int32)[None, :]
    running = jnp.cumsum(owner_table.astype(jnp.int32), axis=0) - 1
    rank_in = jnp.sum(jnp.where(owner_table, running, 0), axis=1)
    owned_here = owner_of == my_index
    target = jnp.where(owned_here, rank_in, OWN_CAP)
    chosen = (
        jnp.zeros((OWN_CAP,), jnp.int32)
        .at[target]
        .set(jnp.arange(requests, dtype=jnp.int32), mode="drop")
    )
    filled = jnp.zeros((OWN_CAP,), jnp.int32).at[target].set(1, mode="drop")
    local_slot = storage_row_of[chosen] - my_index * owner_partial
    slot_pick = jnp.where(
        local_slot[:, None] == jnp.arange(owner_partial, dtype=jnp.int32)[None, :],
        filled[:, None],
        0,
    ).astype(jnp.float32)
    selected_rows = everyone[:, chosen, :]
    reduced_input = jnp.einsum(
        "ldu,hun->ldhn", selected_rows, adapter_down_weight, preferred_element_type=jnp.float32
    )
    rank_part = jnp.sum(reduced_input * slot_pick[None, :, :, None], axis=2)
    spread = jnp.where(
        owned_here[None, :, None], rank_part[:, jnp.minimum(rank_in, OWN_CAP - 1), :], 0.0
    )
    rank_full = lax.psum(spread, ("replica", "tensor"))
    rank_values = rank_full.astype(jnp.bfloat16)
    selected_up_rows = adapter_up_weight[storage_row_of]
    adapter_delta = jnp.einsum(
        "ajz,jzt->ajt", rank_values, selected_up_rows, preferred_element_type=jnp.float32
    )
    return (base_output + adapter_scale * adapter_delta).astype(jnp.bfloat16)


def solution(mesh):
    in_specs = (
        P(None, "replica", "tensor"),
        P("tensor", "replica"),
        P("replica", "tensor", None),
        P(None, None, ("replica", "tensor")),
        P(),
        P(),
    )
    out_specs = P(None, None, ("replica", "tensor"))
    blocks = mesh.shape["replica"] == 8 and mesh.shape["tensor"] == 4
    return jax.shard_map(
        on_device_blocks if blocks else on_device,
        mesh=mesh,
        in_specs=in_specs,
        out_specs=out_specs,
        check_vma=False,
    )
```

```python
import functools

import jax
import jax.numpy as jnp
from jax import lax
from jax.experimental import pallas as pl
from jax.experimental.pallas import tpu as pltpu
from jax.sharding import PartitionSpec as P

OWN_CAP = 48


adapter_scale = 0.5

MIB = 2**20
WIDE = 256
VMEM = pl.BlockSpec(memory_space=pltpu.VMEM)
HBM = pl.BlockSpec(memory_space=pltpu.HBM)


def params(mib):
    return pltpu.CompilerParams(vmem_limit_bytes=mib * MIB)


def stack_rows(parts, rows_ref):
    at = 0
    for part in parts:
        steps, requests, feats = part.shape
        rows_ref[pl.ds(at, steps * requests), :] = part[...].reshape(steps * requests, feats)
        at += steps * requests


def fetch(weight, out, sems, flips):
    cols = out.shape[-1]
    mine = lax.axis_index("tensor")
    copies = []
    for slot, bits in enumerate(flips):
        chunk = pl.ds(pl.multiple_of((mine ^ bits) * cols, cols), cols)
        copies.append(pltpu.make_async_copy(weight.at[:, chunk], out.at[slot], sems.at[slot]))
    for copy in copies:
        copy.start()
    return copies


def turned(row):
    n = row.shape[1]
    same = lax.broadcasted_iota(jnp.int32, (n, n), 0) == lax.broadcasted_iota(jnp.int32, (n, n), 1)
    return jnp.sum(jnp.where(same, row, 0), axis=1, keepdims=True)


def load_kernel(replicas, steps, adapters, weight, request, storage, out, where, inner, sems):
    copies = fetch(weight, out, sems, (1, 3))
    me, mine = lax.axis_index("replica"), lax.axis_index("tensor")
    requests = request.shape[0]
    stored = turned(storage[...].reshape(1, storage.shape[0]))
    count = stored.shape[0]
    asked = lax.broadcasted_iota(jnp.int32, (count, requests), 0) == request[...].reshape(1, requests)
    slot_row = jnp.sum(jnp.where(asked, stored, 0), axis=0, keepdims=True)
    slot = turned(slot_row)

    def owner_of(slots):
        return sum((slots >= first * adapters).astype(jnp.int32) for first in range(1, replicas))

    owner = owner_of(slot)
    square = (requests, requests)
    earlier = lax.broadcasted_iota(jnp.int32, square, 1) < lax.broadcasted_iota(jnp.int32, square, 0)
    order = jnp.sum(jnp.where(earlier & (owner_of(slot_row) == owner), 1, 0), axis=1, keepdims=True)
    half = steps // 2
    place = owner * (steps * OWN_CAP) + order
    column = (owner ^ me) * (half * OWN_CAP) + order
    own = requests // replicas
    for replica in range(replicas):
        mine_here = slice(replica * own, (replica + 1) * own)
        for step in range(steps):
            rows = pl.ds((replica * steps + step) * own, own)
            where[rows, 0:1] = slot[mine_here]
            where[rows, 1:2] = place[mine_here] + step * OWN_CAP
            where[rows, 2:3] = column[mine_here] + (step % half) * OWN_CAP
    inner[...] = jnp.where((mine == 1) | (mine == 2), jnp.ones_like(inner), jnp.zeros_like(inner))
    for copy in copies:
        copy.wait()


def outer_dots(rows, weight, near, mid):
    cols = mid.shape[-1]
    for at in range(0, cols, WIDE):
        where = pl.ds(at, WIDE)
        near[0, :, where] = jnp.dot(
            rows[...], weight[0, :, where], preferred_element_type=jnp.float32
        ).astype(near.dtype)
    for at in range(0, cols, WIDE):
        where = pl.ds(at, WIDE)
        value = jnp.dot(
            rows[...], weight[1, :, where], preferred_element_type=jnp.float32
        ).astype(near.dtype)
        near[1, :, where] = value
        mid[:, where] = value


def outer_kernel(n, *refs):
    parts, weight, near, mid, rows = refs[:n], *refs[n:]
    stack_rows(parts, rows)
    outer_dots(rows, weight, near, mid)


def inner_dots(rows, weight, far, own):
    cols = own.shape[-1]
    for slot, out in enumerate((far, own)):
        for at in range(0, cols, WIDE):
            where = pl.ds(at, WIDE)
            out[:, where] = jnp.dot(rows[...], weight[slot, :, where], preferred_element_type=jnp.float32)


def first_inner_kernel(n, *refs):
    parts, whole, far, own, weight, rows, sems = refs[:n], *refs[n:]
    copies = fetch(whole, weight, sems, (2, 0))
    stack_rows(parts, rows)
    for copy in copies:
        copy.wait()
    inner_dots(rows, weight, far, own)


def inner_kernel(n, *refs):
    parts, weight, far, own, rows = refs[:n], *refs[n:]
    stack_rows(parts, rows)
    inner_dots(rows, weight, far, own)


def rank_kernel(order, before, n, *refs):
    parts, rest, rows = refs[:n], refs[n:-1], refs[-1]
    down, where, out = rest[0], rest[1], rest[-1]
    me = lax.axis_index("replica")
    adapters, rank, feats = down.shape
    stack_rows(parts, rows)
    total = rows.shape[0]
    block = total // len(order)
    starts = [pl.multiple_of((me ^ k) * block, block) for k in order]
    reduced = lax.dot_general(
        rows[...],
        down[...].reshape(adapters * rank, feats),
        (((1,), (1,)), ((), ())),
        preferred_element_type=jnp.float32,
    )
    here = jnp.concatenate([where[pl.ds(at, block), :] for at in starts], axis=0)
    local = here[:, 0:1] - me * adapters
    adapter_of = lax.broadcasted_iota(jnp.int32, (total, adapters * rank), 1) // rank
    picked = jnp.where(adapter_of == local, reduced, 0.0)
    width = adapters * rank
    while width > rank:
        width //= 2
        picked = picked[:, :width] + picked[:, width:]
    half = out.shape[0]
    packed = 2 * half
    place = here[:, 1:2] - me * packed
    chosen = (lax.broadcasted_iota(jnp.int32, (total, packed), 1) == place).astype(jnp.float32)
    packed_rank = lax.dot_general(
        chosen,
        picked,
        (((0,), (0,)), ((), ())),
        preferred_element_type=jnp.float32,
        precision=lax.Precision.HIGHEST,
    )
    value = jnp.concatenate([packed_rank[:half], packed_rank[half:]], axis=1)
    out[...] = value + rest[2][...] if before else value


def up_kernel(packed_rank, up, where, out):
    total = where.shape[0]
    slot, column = where[:, 0:1], where[:, 2:3]
    adapters, rank, cols = up.shape
    owners, held, _ = packed_rank.shape
    chosen = (
        lax.broadcasted_iota(jnp.int32, (total, owners * held), 1) == column
    ).astype(jnp.bfloat16)
    both = jnp.dot(
        chosen, packed_rank[...].reshape(owners * held, 2 * rank), preferred_element_type=jnp.float32
    )
    early_rows = total // owners // 2
    late = (lax.broadcasted_iota(jnp.int32, (total, rank), 0) // early_rows) % 2
    rank_rows = jnp.where(late == 1, both[:, rank:], both[:, :rank])
    group = 8
    wide = jnp.concatenate([rank_rows] * group, axis=1).astype(jnp.bfloat16)
    adapter_of = lax.broadcasted_iota(jnp.int32, (total, group * rank), 1) // rank
    local = slot - adapter_of
    out[...] = jnp.zeros_like(out)

    def step(g, carry):
        spread = jnp.where(local == g * group, wide, jnp.zeros_like(wide))
        weight = up[pl.ds(g * group, group)].reshape(group * rank, cols)
        out[...] += jnp.dot(spread, weight, preferred_element_type=jnp.float32)
        return carry

    lax.fori_loop(0, adapters // group, step, 0)
    out[...] = adapter_scale * out[...]


def finish_kernel(pieces, *refs):
    out, delta = refs[-1], refs[-2]
    steps, _, cols = out.shape
    me = lax.axis_index("replica")
    at = 0
    for order in pieces:
        own, near, far, mid = refs[at : at + 4]
        at += 4
        rows = own.shape[0] // len(order)
        requests = rows // steps
        for i, k in enumerate(order):
            here = pl.ds(i * rows, rows)
            who = me ^ k
            total = own[here, :] + near[0, here, :].astype(jnp.float32)
            total += far[here, :].astype(jnp.float32) + mid[here, :].astype(jnp.float32)
            total += delta[pl.ds(pl.multiple_of(who * rows, rows), rows), :]
            out[:, pl.ds(pl.multiple_of(who * requests, requests), requests), :] = total.astype(
                out.dtype
            ).reshape(steps, requests, cols)


def flip(size, bits):
    return [(i, i ^ bits) for i in range(size)]


def on_device_blocks(
    attention_output,
    output_weight,
    adapter_down_weight,
    adapter_up_weight,
    request_adapter,
    adapter_storage_row,
):
    replicas, tensors = lax.axis_size("replica"), lax.axis_size("tensor")
    steps, own_requests, feats = attention_output.shape
    cols = output_weight.shape[1] // tensors
    adapters_here, _, rank = adapter_down_weight.shape
    requests = request_adapter.shape[0]
    rows = steps * own_requests
    half = steps // 2

    def swap(value, bits):
        return lax.ppermute(value, "replica", flip(replicas, bits))

    def along(value, bits):
        return lax.ppermute(value, "tensor", flip(tensors, bits))

    passed = []

    def tie(*values):
        held = lax.optimization_barrier((*values, *passed))[: len(values)]
        return held[0] if len(values) == 1 else held

    def done(*values):
        passed[:] = values

    def wait(*values):
        passed.extend(values)

    def cost(n, width):
        return pl.CostEstimate(flops=n * width, bytes_accessed=n, transcendentals=0)

    held = pltpu.VMEM((2, feats, cols), jnp.bfloat16)
    copies = pltpu.SemaphoreType.DMA((2,))

    def outer(parts, weight):
        n = sum(p.shape[0] * p.shape[1] for p in parts)
        return pl.pallas_call(
            functools.partial(outer_kernel, len(parts)),
            out_shape=[
                jax.ShapeDtypeStruct((2, n, cols), jnp.bfloat16),
                jax.ShapeDtypeStruct((n, cols), jnp.bfloat16),
            ],
            in_specs=[VMEM] * (len(parts) + 1),
            out_specs=[VMEM, VMEM],
            scratch_shapes=[pltpu.VMEM((n, feats), jnp.bfloat16)],
            compiler_params=params(8),
            cost_estimate=cost(n, 2 * cols),
        )(*parts, weight)

    def inside(parts, weight, first=False):
        n = sum(p.shape[0] * p.shape[1] for p in parts)
        return pl.pallas_call(
            functools.partial(first_inner_kernel if first else inner_kernel, len(parts)),
            out_shape=[jax.ShapeDtypeStruct((n, cols), jnp.float32)] * 2 + [held] * first,
            in_specs=[VMEM] * len(parts) + [HBM if first else VMEM],
            out_specs=[VMEM] * (2 + first),
            scratch_shapes=[pltpu.VMEM((n, feats), jnp.bfloat16)] + [copies] * first,
            compiler_params=params(8),
            cost_estimate=cost(n, 2 * cols),
        )(*parts, weight)

    down = jnp.transpose(adapter_down_weight, (0, 2, 1))

    def ranked(order, parts, *before):
        n = rows * len(order)
        return pl.pallas_call(
            functools.partial(rank_kernel, order, len(before) > 0, len(parts)),
            out_shape=jax.ShapeDtypeStruct((half * OWN_CAP, 2 * rank), jnp.float32),
            in_specs=[VMEM] * (len(parts) + 2 + len(before)),
            out_specs=VMEM,
            scratch_shapes=[pltpu.VMEM((n, feats), jnp.bfloat16)],
            compiler_params=params(10),
            cost_estimate=cost(n, adapters_here * rank),
        )(*parts, down, where, *before)

    def pass_on(far, near_in):
        both = far + jnp.where(inner > 0, near_in[1].astype(jnp.float32), 0.0)
        both = both.astype(jnp.bfloat16)
        return along(both, 2), both

    def across(mid):
        return lax.ppermute(mid, "tensor", [(1, 2), (2, 1)])

    x0 = attention_output
    x1, x2, x4 = swap(x0, 1), swap(x0, 2), swap(x0, 4)
    weight = pltpu.with_memory_space_constraint(output_weight, pltpu.HBM)
    held_out, where, inner = pl.pallas_call(
        functools.partial(load_kernel, replicas, steps, adapters_here),
        out_shape=[
            held,
            jax.ShapeDtypeStruct((replicas * rows, 8), jnp.int32),
            jax.ShapeDtypeStruct((1, cols), jnp.float32),
        ],
        in_specs=[HBM, VMEM, VMEM],
        out_specs=[VMEM] * 3,
        scratch_shapes=[copies],
        compiler_params=params(4),
    )(weight, request_adapter, adapter_storage_row)
    near0, mid0 = outer([x0, x1], held_out)
    done(near0)
    near0_in, mid0_in = along(near0, 1), across(mid0)
    far0, own0, held_in = inside([tie(x0), x1], weight, True)
    done(own0)
    packed = ranked((0, 1), [tie(x0), x1])
    done(packed)
    far0_in, sent = pass_on(far0, tie(near0_in))
    wait(sent)

    wait(x2, x4, mid0_in)
    x2, x4 = tie(x2, x4)
    x3, x6a = swap(x2, 1), swap(x2[:half], 4)
    x5, x6b = swap(x4, 1), swap(x4[half:], 2)
    wait(x3)
    near1, mid1 = outer([tie(x2), x3], held_out)
    done(near1)
    near1_in = along(near1, 1)
    wait(x5)
    mid1_in = across(tie(mid1))
    far1, own1 = inside([tie(x2), x3], held_in)
    done(own1)
    packed = ranked((2, 3), [tie(x2), x3], packed)
    done(packed)

    wait(x6a, x6b)
    x6a, x6b = tie(x6a, x6b)
    x7a, x7b = swap(x6a, 1), swap(x6b, 1)
    near2, mid2 = outer([tie(x4), x5], held_out)
    done(near2)
    wait(x7a, x7b, far0_in)
    near2_in, mid2_in = along(tie(near2), 1), across(tie(mid2))
    packed = ranked((4, 5, 6, 7), [tie(x4), x5, x6a, x6b, x7a, x7b], packed)
    done(packed)
    packed_in = along(packed, 1)
    wait(near1_in, mid1_in)
    far1_in, sent = pass_on(far1, tie(near1_in))
    wait(sent)
    near3, mid3 = outer([tie(x6a), x6b, x7a, x7b], held_out)
    done(near3)
    near3_in = along(near3, 1)
    wait(packed_in)
    packed = packed + tie(packed_in)
    done(packed)
    packed_in = along(packed, 2)
    far2, own2 = inside([tie(x4), x5], held_in)
    done(own2)
    wait(mid2_in, near2_in)
    mid3_in = across(tie(mid3))
    far2_in, sent = pass_on(far2, tie(near2_in))
    wait(sent)
    far3, own3 = inside([tie(x6a), x6b, x7a, x7b], held_in)
    done(own3)
    wait(packed_in)
    ranks = (packed + tie(packed_in)).astype(jnp.bfloat16)[None]
    done(ranks)
    got = swap(ranks, 1)
    wait(far1_in, got)
    ranks = jnp.concatenate([ranks, tie(got)], axis=0)
    done(ranks)
    got = swap(ranks, 2)
    wait(near3_in)
    far3_in, sent = pass_on(far3, tie(near3_in))
    wait(sent, got, far2_in)
    ranks = jnp.concatenate([ranks, tie(got)], axis=0)
    done(ranks)
    got = swap(ranks, 4)
    wait(got, mid3_in)
    ranks = jnp.concatenate([ranks, tie(got)], axis=0)

    delta = pl.pallas_call(
        up_kernel,
        out_shape=jax.ShapeDtypeStruct((replicas * rows, cols), jnp.float32),
        in_specs=[VMEM] * 3,
        out_specs=VMEM,
        compiler_params=params(12),
        cost_estimate=pl.CostEstimate(
            flops=2 * replicas * rows * cols * adapter_up_weight.shape[0] * rank,
            bytes_accessed=4 * MIB,
            transcendentals=0,
        ),
    )(ranks, adapter_up_weight, where)

    pieces = [(0, 1), (2, 3), (4, 5), (6, 7)]
    shares = [
        (own0, near0_in, far0_in, mid0_in),
        (own1, near1_in, far1_in, mid1_in),
        (own2, near2_in, far2_in, mid2_in),
        (own3, near3_in, far3_in, mid3_in),
    ]
    return pl.pallas_call(
        functools.partial(finish_kernel, pieces),
        out_shape=jax.ShapeDtypeStruct((steps, requests, cols), jnp.bfloat16),
        in_specs=[VMEM] * 17,
        out_specs=VMEM,
        compiler_params=params(12),
    )(*[ref for share in shares for ref in share], delta)


def on_device(
    attention_output,
    output_weight,
    adapter_down_weight,
    adapter_up_weight,
    request_adapter,
    adapter_storage_row,
):
    replicas = lax.axis_size("replica")
    my_index = lax.axis_index("replica")
    owner_partial = adapter_down_weight.shape[0]
    requests = request_adapter.shape[0]
    everyone = lax.all_gather(attention_output, "replica", axis=1, tiled=True)
    partial_sums = jnp.einsum(
        "sif,fc->sic", everyone, output_weight, preferred_element_type=jnp.float32
    )
    base_output = lax.psum_scatter(partial_sums, "tensor", scatter_dimension=2, tiled=True)
    adapter_ids = jnp.arange(adapter_storage_row.shape[0], dtype=jnp.int32)
    storage_row_of = jnp.sum(
        jnp.where(
            request_adapter[:, None] == adapter_ids[None, :], adapter_storage_row[None, :], 0
        ),
        axis=1,
    )
    owner_of = storage_row_of // owner_partial
    owner_table = owner_of[:, None] == jnp.arange(replicas, dtype=jnp.int32)[None, :]
    running = jnp.cumsum(owner_table.astype(jnp.int32), axis=0) - 1
    rank_in = jnp.sum(jnp.where(owner_table, running, 0), axis=1)
    owned_here = owner_of == my_index
    target = jnp.where(owned_here, rank_in, OWN_CAP)
    chosen = (
        jnp.zeros((OWN_CAP,), jnp.int32)
        .at[target]
        .set(jnp.arange(requests, dtype=jnp.int32), mode="drop")
    )
    filled = jnp.zeros((OWN_CAP,), jnp.int32).at[target].set(1, mode="drop")
    local_slot = storage_row_of[chosen] - my_index * owner_partial
    slot_pick = jnp.where(
        local_slot[:, None] == jnp.arange(owner_partial, dtype=jnp.int32)[None, :],
        filled[:, None],
        0,
    ).astype(jnp.float32)
    selected_rows = everyone[:, chosen, :]
    reduced_input = jnp.einsum(
        "ldu,hun->ldhn", selected_rows, adapter_down_weight, preferred_element_type=jnp.float32
    )
    rank_part = jnp.sum(reduced_input * slot_pick[None, :, :, None], axis=2)
    spread = jnp.where(
        owned_here[None, :, None], rank_part[:, jnp.minimum(rank_in, OWN_CAP - 1), :], 0.0
    )
    rank_full = lax.psum(spread, ("replica", "tensor"))
    rank_values = rank_full.astype(jnp.bfloat16)
    selected_up_rows = adapter_up_weight[storage_row_of]
    adapter_delta = jnp.einsum(
        "ajz,jzt->ajt", rank_values, selected_up_rows, preferred_element_type=jnp.float32
    )
    return (base_output + adapter_scale * adapter_delta).astype(jnp.bfloat16)


def solution(mesh):
    in_specs = (
        P(None, "replica", "tensor"),
        P("tensor", "replica"),
        P("replica", "tensor", None),
        P(None, None, ("replica", "tensor")),
        P(),
        P(),
    )
    out_specs = P(None, None, ("replica", "tensor"))
    blocks = mesh.shape["replica"] == 8 and mesh.shape["tensor"] == 4
    return jax.shard_map(
        on_device_blocks if blocks else on_device,
        mesh=mesh,
        in_specs=in_specs,
        out_specs=out_specs,
        check_vma=False,
    )
```

```python
import functools

import jax
import jax.numpy as jnp
from jax import lax
from jax.experimental import pallas as pl
from jax.experimental.pallas import tpu as pltpu
from jax.sharding import PartitionSpec as P

OWN_CAP = 48


adapter_scale = 0.5

MIB = 2**20
WIDE = 256
VMEM = pl.BlockSpec(memory_space=pltpu.VMEM)
HBM = pl.BlockSpec(memory_space=pltpu.HBM)
ANY = pl.BlockSpec(memory_space=pl.ANY)


def params(mib):
    return pltpu.CompilerParams(vmem_limit_bytes=mib * MIB)


def stack_rows(parts, rows_ref):
    at = 0
    for part in parts:
        steps, requests, feats = part.shape
        rows_ref[pl.ds(at, steps * requests), :] = part[...].reshape(steps * requests, feats)
        at += steps * requests


def fetch(weight, out, sems, flips):
    cols = out.shape[-1]
    mine = lax.axis_index("tensor")
    copies = []
    for slot, bits in enumerate(flips):
        chunk = pl.ds(pl.multiple_of((mine ^ bits) * cols, cols), cols)
        copies.append(pltpu.make_async_copy(weight.at[:, chunk], out.at[slot], sems.at[slot]))
    for copy in copies:
        copy.start()
    return copies


def turned(row):
    n = row.shape[1]
    same = lax.broadcasted_iota(jnp.int32, (n, n), 0) == lax.broadcasted_iota(jnp.int32, (n, n), 1)
    return jnp.sum(jnp.where(same, row, 0), axis=1, keepdims=True)


def load_kernel(replicas, steps, adapters, weight, request_in, storage_in, out, where, request, storage, sems, small):
    asked_for = pltpu.make_async_copy(request_in, request, small.at[0])
    stored_at = pltpu.make_async_copy(storage_in, storage, small.at[1])
    asked_for.start()
    stored_at.start()
    copies = fetch(weight, out, sems, (1, 3))
    me = lax.axis_index("replica")
    asked_for.wait()
    stored_at.wait()
    requests = request.shape[0]
    stored = turned(storage[...].reshape(1, storage.shape[0]))
    count = stored.shape[0]
    asked = lax.broadcasted_iota(jnp.int32, (count, requests), 0) == request[...].reshape(1, requests)
    slot_row = jnp.sum(jnp.where(asked, stored, 0), axis=0, keepdims=True)
    slot = turned(slot_row)

    def owner_of(slots):
        return sum((slots >= first * adapters).astype(jnp.int32) for first in range(1, replicas))

    owner = owner_of(slot)
    square = (requests, requests)
    earlier = lax.broadcasted_iota(jnp.int32, square, 1) < lax.broadcasted_iota(jnp.int32, square, 0)
    order = jnp.sum(jnp.where(earlier & (owner_of(slot_row) == owner), 1, 0), axis=1, keepdims=True)
    half = steps // 2
    place = owner * (steps * OWN_CAP) + order
    column = (owner ^ me) * (half * OWN_CAP) + order
    own = requests // replicas
    for replica in range(replicas):
        mine_here = slice(replica * own, (replica + 1) * own)
        for step in range(steps):
            rows = pl.ds((replica * steps + step) * own, own)
            where[rows, 0:1] = slot[mine_here]
            where[rows, 1:2] = place[mine_here] + step * OWN_CAP
            where[rows, 2:3] = column[mine_here] + (step % half) * OWN_CAP
    for copy in copies:
        copy.wait()


def outer_dots(rows, weight, near):
    cols = near.shape[-1]
    for slot in range(2):
        for at in range(0, cols, WIDE):
            where = pl.ds(at, WIDE)
            near[slot, :, where] = jnp.dot(
                rows[...], weight[slot, :, where], preferred_element_type=jnp.float32
            ).astype(near.dtype)


def outer_kernel(n, *refs):
    parts, weight, near, rows = refs[:n], *refs[n:]
    stack_rows(parts, rows)
    outer_dots(rows, weight, near)


def inner_dots(rows, weight, far, own):
    cols = own.shape[-1]
    for slot, out in enumerate((far, own)):
        for at in range(0, cols, WIDE):
            where = pl.ds(at, WIDE)
            out[:, where] = jnp.dot(rows[...], weight[slot, :, where], preferred_element_type=jnp.float32)


def first_inner_kernel(n, *refs):
    parts, whole, far, own, weight, rows, sems = refs[:n], *refs[n:]
    copies = fetch(whole, weight, sems, (2, 0))
    stack_rows(parts, rows)
    for copy in copies:
        copy.wait()
    inner_dots(rows, weight, far, own)


def inner_kernel(n, *refs):
    parts, weight, far, own, rows = refs[:n], *refs[n:]
    stack_rows(parts, rows)
    inner_dots(rows, weight, far, own)


def rank_kernel(order, before, n, *refs):
    parts, rest, rows = refs[:n], refs[n:-1], refs[-1]
    down, where, out = rest[0], rest[1], rest[-1]
    me = lax.axis_index("replica")
    adapters, rank, feats = down.shape
    stack_rows(parts, rows)
    total = rows.shape[0]
    block = total // len(order)
    starts = [pl.multiple_of((me ^ k) * block, block) for k in order]
    reduced = lax.dot_general(
        rows[...],
        down[...].reshape(adapters * rank, feats),
        (((1,), (1,)), ((), ())),
        preferred_element_type=jnp.float32,
    )
    here = jnp.concatenate([where[pl.ds(at, block), :] for at in starts], axis=0)
    local = here[:, 0:1] - me * adapters
    adapter_of = lax.broadcasted_iota(jnp.int32, (total, adapters * rank), 1) // rank
    picked = jnp.where(adapter_of == local, reduced, 0.0)
    width = adapters * rank
    while width > rank:
        width //= 2
        picked = picked[:, :width] + picked[:, width:]
    half = out.shape[0]
    packed = 2 * half
    place = here[:, 1:2] - me * packed
    chosen = (lax.broadcasted_iota(jnp.int32, (total, packed), 1) == place).astype(jnp.float32)
    packed_rank = lax.dot_general(
        chosen,
        picked,
        (((0,), (0,)), ((), ())),
        preferred_element_type=jnp.float32,
        precision=lax.Precision.HIGHEST,
    )
    value = jnp.concatenate([packed_rank[:half], packed_rank[half:]], axis=1)
    out[...] = value + rest[2][...] if before else value


def up_kernel(first, before, *refs):
    ranks, rest = refs[: -4 - before], refs[-4 - before :]
    up, where, out = rest[0], rest[1], rest[-2]
    wide = rest[-1]
    me = lax.axis_index("replica")
    total, cols = out.shape
    rank = up.shape[1]
    held = ranks[0].shape[1]
    packed_rank = jnp.concatenate([r[...].reshape(-1, r.shape[-1]) for r in ranks], axis=0)
    owners = packed_rank.shape[0] // held
    slot, column = where[:, 0:1], where[:, 2:3] - first * held
    chosen = (lax.broadcasted_iota(jnp.int32, (total, owners * held), 1) == column).astype(jnp.bfloat16)
    both = jnp.dot(chosen, packed_rank, preferred_element_type=jnp.float32)
    early_rows = total // lax.axis_size("replica") // 2
    late = (lax.broadcasted_iota(jnp.int32, (total, rank), 0) // early_rows) % 2
    rank_rows = adapter_scale * jnp.where(late == 1, both[:, rank:], both[:, :rank])
    group = wide.shape[1] // rank
    wide[...] = jnp.concatenate([rank_rows] * group, axis=1).astype(jnp.bfloat16)
    adapter_of = slot - lax.broadcasted_iota(jnp.int32, wide.shape, 1) // rank
    made = rest[2][...] if before else None
    for owner in range(owners):
        at = (me ^ (first + owner)) * group
        spread = jnp.where(adapter_of == at, wide[...], jnp.zeros_like(wide))
        weight = up[pl.ds(at, group)].reshape(group * rank, cols)
        part = jnp.dot(spread, weight, preferred_element_type=jnp.float32)
        made = part if made is None else made + part
    out[...] = made


def finish_kernel(pieces, *refs):
    out, delta = refs[-1], refs[-2]
    steps, _, cols = out.shape
    me = lax.axis_index("replica")
    at = 0
    for order in pieces:
        own, near, far = refs[at : at + 3]
        at += 3
        rows = own.shape[0] // len(order)
        requests = rows // steps
        for i, k in enumerate(order):
            here = pl.ds(i * rows, rows)
            who = me ^ k
            total = own[here, :] + near[0, here, :].astype(jnp.float32)
            total += far[here, :].astype(jnp.float32)
            total += delta[pl.ds(pl.multiple_of(who * rows, rows), rows), :]
            out[:, pl.ds(pl.multiple_of(who * requests, requests), requests), :] = total.astype(
                out.dtype
            ).reshape(steps, requests, cols)


def flip(size, bits):
    return [(i, i ^ bits) for i in range(size)]


def on_device_blocks(
    attention_output,
    output_weight,
    adapter_down_weight,
    adapter_up_weight,
    request_adapter,
    adapter_storage_row,
):
    replicas, tensors = lax.axis_size("replica"), lax.axis_size("tensor")
    steps, own_requests, feats = attention_output.shape
    cols = output_weight.shape[1] // tensors
    adapters_here, _, rank = adapter_down_weight.shape
    requests = request_adapter.shape[0]
    rows = steps * own_requests
    half = steps // 2

    def swap(value, bits):
        return lax.ppermute(value, "replica", flip(replicas, bits))

    def along(value, bits):
        return lax.ppermute(value, "tensor", flip(tensors, bits))

    passed = []

    def tie(*values):
        held = lax.optimization_barrier((*values, *passed))[: len(values)]
        return held[0] if len(values) == 1 else held

    def done(*values):
        passed[:] = values

    def wait(*values):
        passed.extend(values)

    def cost(n, width):
        return pl.CostEstimate(flops=2 * n * feats * width, bytes_accessed=2 * n * feats, transcendentals=0)

    held = pltpu.VMEM((2, feats, cols), jnp.bfloat16)
    copies = pltpu.SemaphoreType.DMA((2,))

    def outer(parts, weight):
        n = sum(p.shape[0] * p.shape[1] for p in parts)
        return pl.pallas_call(
            functools.partial(outer_kernel, len(parts)),
            out_shape=jax.ShapeDtypeStruct((2, n, cols), jnp.bfloat16),
            in_specs=[VMEM] * (len(parts) + 1),
            out_specs=VMEM,
            scratch_shapes=[pltpu.VMEM((n, feats), jnp.bfloat16)],
            compiler_params=params(8),
            cost_estimate=cost(n, 2 * cols),
        )(*parts, weight)

    def inside(parts, weight, first=False):
        n = sum(p.shape[0] * p.shape[1] for p in parts)
        return pl.pallas_call(
            functools.partial(first_inner_kernel if first else inner_kernel, len(parts)),
            out_shape=[jax.ShapeDtypeStruct((n, cols), jnp.float32)] * 2 + [held] * first,
            in_specs=[VMEM] * len(parts) + [HBM if first else VMEM],
            out_specs=[VMEM] * (2 + first),
            scratch_shapes=[pltpu.VMEM((n, feats), jnp.bfloat16)] + [copies] * first,
            compiler_params=params(8),
            cost_estimate=cost(n, 2 * cols),
        )(*parts, weight)

    down = jnp.transpose(adapter_down_weight, (0, 2, 1))

    def ranked(order, parts, *before):
        n = rows * len(order)
        return pl.pallas_call(
            functools.partial(rank_kernel, order, len(before) > 0, len(parts)),
            out_shape=jax.ShapeDtypeStruct((half * OWN_CAP, 2 * rank), jnp.float32),
            in_specs=[VMEM] * (len(parts) + 2 + len(before)),
            out_specs=VMEM,
            scratch_shapes=[pltpu.VMEM((n, feats), jnp.bfloat16)],
            compiler_params=params(10),
            cost_estimate=cost(n, adapters_here * rank),
        )(*parts, down, where, *before)

    def pass_on(far, near_in):
        return (far + near_in[1].astype(jnp.float32)).astype(jnp.bfloat16)

    x0 = attention_output
    x1, x2, x4 = swap(x0, 1), swap(x0, 2), swap(x0, 4)
    weight = pltpu.with_memory_space_constraint(output_weight, pltpu.HBM)
    held_out, where = pl.pallas_call(
        functools.partial(load_kernel, replicas, steps, adapters_here),
        out_shape=[held, jax.ShapeDtypeStruct((replicas * rows, 8), jnp.int32)],
        in_specs=[HBM] * 3,
        out_specs=[VMEM] * 2,
        scratch_shapes=[
            pltpu.VMEM(request_adapter.shape, jnp.int32),
            pltpu.VMEM(adapter_storage_row.shape, jnp.int32),
            copies,
            copies,
        ],
        compiler_params=params(4),
    )(weight, *(pltpu.with_memory_space_constraint(v, pltpu.HBM) for v in (request_adapter, adapter_storage_row)))
    near0 = outer([x0, x1], held_out)
    done(near0)
    near0_in = along(near0, 1)
    far0, own0, held_in = inside([tie(x0), x1], weight, True)
    done(own0)

    wait(x2, x4, near0_in)
    x2, x4 = tie(x2, x4)
    x3, x5 = swap(x2, 1), swap(x4, 1)
    x6a, x6b = swap(x2[:half], 4), swap(x4[half:], 2)
    near1 = outer([x2, x3, x4, x5], held_out)
    done(near1)
    near1_in = along(near1, 1)
    far0_out = pass_on(far0, tie(near0_in))
    far0_in = along(far0_out, 2)
    wait(far0_out)
    far1, own1 = inside([tie(x2), x3, x4, x5], held_in)
    done(own1)
    packed = ranked((0, 1, 2, 3, 4, 5), [tie(x0), x1, x2, x3, x4, x5])
    done(packed)

    wait(x6a, x6b)
    x6a, x6b = tie(x6a, x6b)
    x7a, x7b = swap(x6a, 1), swap(x6b, 1)
    packed = ranked((6, 7), [x6a, x6b, x7a, x7b], packed)
    done(packed)
    packed_in = along(packed, 1)
    near2 = outer([tie(x6a), x6b, x7a, x7b], held_out)
    done(near2)
    near2_in = along(near2, 1)
    wait(far0_in)
    far1_out = pass_on(far1, tie(near1_in))
    wait(far1_out, packed_in)
    packed = packed + tie(packed_in)
    done(packed)
    packed_in = along(packed, 2)
    far1_in = along(far1_out, 2)
    far2, own2 = inside([tie(x6a), x6b, x7a, x7b], held_in)
    done(own2)
    far2_out = pass_on(far2, tie(near2_in))
    far2_in = along(far2_out, 2)
    wait(far2_out)

    def up(first, ranks, *before):
        return pl.pallas_call(
            functools.partial(up_kernel, first, len(before)),
            out_shape=jax.ShapeDtypeStruct((replicas * rows, cols), jnp.float32),
            in_specs=[VMEM] * (len(ranks) + 2 + len(before)),
            out_specs=VMEM,
            scratch_shapes=[pltpu.VMEM((replicas * rows, adapters_here * rank), jnp.bfloat16)],
            compiler_params=params(12),
        )(*ranks, adapter_up_weight, where, *before)

    wait(packed_in)
    ranks = (packed + tie(packed_in)).astype(jnp.bfloat16)[None]
    done(ranks)
    got = swap(ranks, 1)
    wait(got)
    ranks = jnp.concatenate([ranks, tie(got)], axis=0)
    done(ranks)
    got2, got4, got6 = (swap(ranks, bits) for bits in (2, 4, 6))
    delta = up(0, [tie(ranks)])
    done(delta)
    wait(got2, got4)
    delta = up(2, [tie(got2), got4], delta)
    done(delta)
    wait(got6, far1_in)
    delta = up(6, [tie(got6)], delta)

    pieces = [(0, 1), (2, 3, 4, 5), (6, 7)]
    arrived = [(own0, near0_in, far0_in), (own1, near1_in, far1_in), (own2, near2_in, far2_in)]
    return pl.pallas_call(
        functools.partial(finish_kernel, pieces),
        out_shape=jax.ShapeDtypeStruct((steps, requests, cols), jnp.bfloat16),
        in_specs=[VMEM] * 10,
        out_specs=VMEM,
        compiler_params=params(12),
    )(*[ref for piece in arrived for ref in piece], delta)


def on_device(
    attention_output,
    output_weight,
    adapter_down_weight,
    adapter_up_weight,
    request_adapter,
    adapter_storage_row,
):
    replicas = lax.axis_size("replica")
    my_index = lax.axis_index("replica")
    owner_partial = adapter_down_weight.shape[0]
    requests = request_adapter.shape[0]
    everyone = lax.all_gather(attention_output, "replica", axis=1, tiled=True)
    partial_sums = jnp.einsum(
        "sif,fc->sic", everyone, output_weight, preferred_element_type=jnp.float32
    )
    base_output = lax.psum_scatter(partial_sums, "tensor", scatter_dimension=2, tiled=True)
    adapter_ids = jnp.arange(adapter_storage_row.shape[0], dtype=jnp.int32)
    storage_row_of = jnp.sum(
        jnp.where(
            request_adapter[:, None] == adapter_ids[None, :], adapter_storage_row[None, :], 0
        ),
        axis=1,
    )
    owner_of = storage_row_of // owner_partial
    owner_table = owner_of[:, None] == jnp.arange(replicas, dtype=jnp.int32)[None, :]
    running = jnp.cumsum(owner_table.astype(jnp.int32), axis=0) - 1
    rank_in = jnp.sum(jnp.where(owner_table, running, 0), axis=1)
    owned_here = owner_of == my_index
    target = jnp.where(owned_here, rank_in, OWN_CAP)
    chosen = (
        jnp.zeros((OWN_CAP,), jnp.int32)
        .at[target]
        .set(jnp.arange(requests, dtype=jnp.int32), mode="drop")
    )
    filled = jnp.zeros((OWN_CAP,), jnp.int32).at[target].set(1, mode="drop")
    local_slot = storage_row_of[chosen] - my_index * owner_partial
    slot_pick = jnp.where(
        local_slot[:, None] == jnp.arange(owner_partial, dtype=jnp.int32)[None, :],
        filled[:, None],
        0,
    ).astype(jnp.float32)
    selected_rows = everyone[:, chosen, :]
    reduced_input = jnp.einsum(
        "ldu,hun->ldhn", selected_rows, adapter_down_weight, preferred_element_type=jnp.float32
    )
    rank_part = jnp.sum(reduced_input * slot_pick[None, :, :, None], axis=2)
    spread = jnp.where(
        owned_here[None, :, None], rank_part[:, jnp.minimum(rank_in, OWN_CAP - 1), :], 0.0
    )
    rank_full = lax.psum(spread, ("replica", "tensor"))
    rank_values = rank_full.astype(jnp.bfloat16)
    selected_up_rows = adapter_up_weight[storage_row_of]
    adapter_delta = jnp.einsum(
        "ajz,jzt->ajt", rank_values, selected_up_rows, preferred_element_type=jnp.float32
    )
    return (base_output + adapter_scale * adapter_delta).astype(jnp.bfloat16)


def solution(mesh):
    in_specs = (
        P(None, "replica", "tensor"),
        P("tensor", "replica"),
        P("replica", "tensor", None),
        P(None, None, ("replica", "tensor")),
        P(),
        P(),
    )
    out_specs = P(None, None, ("replica", "tensor"))
    blocks = mesh.shape["replica"] == 8 and mesh.shape["tensor"] == 4
    return jax.shard_map(
        on_device_blocks if blocks else on_device,
        mesh=mesh,
        in_specs=in_specs,
        out_specs=out_specs,
        check_vma=False,
    )
```

```python
import functools

import jax
import jax.numpy as jnp
from jax import lax
from jax.experimental import pallas as pl
from jax.experimental.pallas import tpu as pltpu
from jax.sharding import PartitionSpec as P

OWN_CAP = 48


adapter_scale = 0.5

MIB = 2**20
WIDE = 256
VMEM = pl.BlockSpec(memory_space=pltpu.VMEM)
HBM = pl.BlockSpec(memory_space=pltpu.HBM)
ANY = pl.BlockSpec(memory_space=pl.ANY)


def params(mib):
    return pltpu.CompilerParams(vmem_limit_bytes=mib * MIB)


def stack_rows(parts, rows_ref):
    at = 0
    for part in parts:
        steps, requests, feats = part.shape
        rows_ref[pl.ds(at, steps * requests), :] = part[...].reshape(steps * requests, feats)
        at += steps * requests


def fetch(weight, out, sems, flips):
    cols = out.shape[-1]
    mine = lax.axis_index("tensor")
    copies = []
    for slot, bits in enumerate(flips):
        chunk = pl.ds(pl.multiple_of((mine ^ bits) * cols, cols), cols)
        copies.append(pltpu.make_async_copy(weight.at[:, chunk], out.at[slot], sems.at[slot]))
    for copy in copies:
        copy.start()
    return copies


def turned(row):
    n = row.shape[1]
    same = lax.broadcasted_iota(jnp.int32, (n, n), 0) == lax.broadcasted_iota(jnp.int32, (n, n), 1)
    return jnp.sum(jnp.where(same, row, 0), axis=1, keepdims=True)


def load_kernel(replicas, steps, adapters, weight, request_in, storage_in, out, where, request, storage, sems, small):
    asked_for = pltpu.make_async_copy(request_in, request, small.at[0])
    stored_at = pltpu.make_async_copy(storage_in, storage, small.at[1])
    asked_for.start()
    stored_at.start()
    copies = fetch(weight, out, sems, (1, 3))
    me = lax.axis_index("replica")
    asked_for.wait()
    stored_at.wait()
    requests = request.shape[0]
    stored = turned(storage[...].reshape(1, storage.shape[0]))
    count = stored.shape[0]
    asked = lax.broadcasted_iota(jnp.int32, (count, requests), 0) == request[...].reshape(1, requests)
    slot_row = jnp.sum(jnp.where(asked, stored, 0), axis=0, keepdims=True)
    slot = turned(slot_row)

    def owner_of(slots):
        return sum((slots >= first * adapters).astype(jnp.int32) for first in range(1, replicas))

    owner = owner_of(slot)
    square = (requests, requests)
    earlier = lax.broadcasted_iota(jnp.int32, square, 1) < lax.broadcasted_iota(jnp.int32, square, 0)
    order = jnp.sum(jnp.where(earlier & (owner_of(slot_row) == owner), 1, 0), axis=1, keepdims=True)
    half = steps // 2
    place = owner * (steps * OWN_CAP) + order
    column = (owner ^ me) * (half * OWN_CAP) + order
    own = requests // replicas
    for replica in range(replicas):
        mine_here = slice(replica * own, (replica + 1) * own)
        for step in range(steps):
            rows = pl.ds((replica * steps + step) * own, own)
            where[rows, 0:1] = slot[mine_here]
            where[rows, 1:2] = place[mine_here] + step * OWN_CAP
            where[rows, 2:3] = column[mine_here] + (step % half) * OWN_CAP
    for copy in copies:
        copy.wait()


def outer_dots(rows, weight, near):
    cols = near.shape[-1]
    for slot in range(2):
        for at in range(0, cols, WIDE):
            where = pl.ds(at, WIDE)
            near[slot, :, where] = jnp.dot(
                rows[...], weight[slot, :, where], preferred_element_type=jnp.float32
            ).astype(near.dtype)


def outer_kernel(n, *refs):
    parts, weight, near, rows = refs[:n], *refs[n:]
    stack_rows(parts, rows)
    outer_dots(rows, weight, near)


def inner_dots(rows, weight, far, own):
    cols = own.shape[-1]
    for slot, out in enumerate((far, own)):
        for at in range(0, cols, WIDE):
            where = pl.ds(at, WIDE)
            out[:, where] = jnp.dot(rows[...], weight[slot, :, where], preferred_element_type=jnp.float32)


def first_inner_kernel(n, *refs):
    parts, whole, far, own, weight, rows, sems = refs[:n], *refs[n:]
    copies = fetch(whole, weight, sems, (2, 0))
    stack_rows(parts, rows)
    for copy in copies:
        copy.wait()
    inner_dots(rows, weight, far, own)


def inner_kernel(n, *refs):
    parts, weight, far, own, rows = refs[:n], *refs[n:]
    stack_rows(parts, rows)
    inner_dots(rows, weight, far, own)


def rank_kernel(blocks, before, n, *refs):
    parts, rest, rows = refs[:n], refs[n:-1], refs[-1]
    down, where, out = rest[0], rest[1], rest[-1]
    me = lax.axis_index("replica")
    adapters, rank, feats = down.shape
    stack_rows(parts, rows)
    total = rows.shape[0]
    whole = where.shape[0] // lax.axis_size("replica")
    here = []
    for (bits, first), part in zip(blocks, parts):
        steps, requests, _ = part.shape
        at = pl.multiple_of((me ^ bits) * whole + first * requests, requests)
        here.append(where[pl.ds(at, steps * requests), :])
    here = jnp.concatenate(here, axis=0)
    reduced = lax.dot_general(
        rows[...],
        down[...].reshape(adapters * rank, feats),
        (((1,), (1,)), ((), ())),
        preferred_element_type=jnp.float32,
    )
    local = here[:, 0:1] - me * adapters
    adapter_of = lax.broadcasted_iota(jnp.int32, (total, adapters * rank), 1) // rank
    picked = jnp.where(adapter_of == local, reduced, 0.0)
    width = adapters * rank
    while width > rank:
        width //= 2
        picked = picked[:, :width] + picked[:, width:]
    half = out.shape[0]
    packed = 2 * half
    place = here[:, 1:2] - me * packed
    chosen = (lax.broadcasted_iota(jnp.int32, (total, packed), 1) == place).astype(jnp.float32)
    packed_rank = lax.dot_general(
        chosen,
        picked,
        (((0,), (0,)), ((), ())),
        preferred_element_type=jnp.float32,
        precision=lax.Precision.HIGHEST,
    )
    value = jnp.concatenate([packed_rank[:half], packed_rank[half:]], axis=1)
    out[...] = value + rest[2][...] if before else value


def up_kernel(first, before, *refs):
    ranks, rest = refs[: -4 - before], refs[-4 - before :]
    up, where, out = rest[0], rest[1], rest[-2]
    wide = rest[-1]
    me = lax.axis_index("replica")
    total, cols = out.shape
    rank = up.shape[1]
    held = ranks[0].shape[1]
    packed_rank = jnp.concatenate([r[...].reshape(-1, r.shape[-1]) for r in ranks], axis=0)
    owners = packed_rank.shape[0] // held
    slot, column = where[:, 0:1], where[:, 2:3] - first * held
    chosen = (lax.broadcasted_iota(jnp.int32, (total, owners * held), 1) == column).astype(jnp.bfloat16)
    both = jnp.dot(chosen, packed_rank, preferred_element_type=jnp.float32)
    early_rows = total // lax.axis_size("replica") // 2
    late = (lax.broadcasted_iota(jnp.int32, (total, rank), 0) // early_rows) % 2
    rank_rows = adapter_scale * jnp.where(late == 1, both[:, rank:], both[:, :rank])
    group = wide.shape[1] // rank
    wide[...] = jnp.concatenate([rank_rows] * group, axis=1).astype(jnp.bfloat16)
    adapter_of = slot - lax.broadcasted_iota(jnp.int32, wide.shape, 1) // rank
    made = rest[2][...] if before else None
    for owner in range(owners):
        at = (me ^ (first + owner)) * group
        spread = jnp.where(adapter_of == at, wide[...], jnp.zeros_like(wide))
        weight = up[pl.ds(at, group)].reshape(group * rank, cols)
        part = jnp.dot(spread, weight, preferred_element_type=jnp.float32)
        made = part if made is None else made + part
    out[...] = made


def finish_kernel(pieces, *refs):
    out, delta = refs[-1], refs[-2]
    steps, requests, cols = out.shape
    replicas = lax.axis_size("replica")
    own_requests = requests // replicas
    me = lax.axis_index("replica")
    for i, blocks in enumerate(pieces):
        own, near, far = refs[3 * i : 3 * i + 3]
        at = 0
        for bits, first, count in blocks:
            rows = count * own_requests
            here = pl.ds(at, rows)
            at += rows
            who = me ^ bits
            total = own[here, :] + near[0, here, :].astype(jnp.float32)
            total += far[here, :].astype(jnp.float32)
            start = pl.multiple_of((who * steps + first) * own_requests, own_requests)
            total += delta[pl.ds(start, rows), :]
            place = pl.ds(pl.multiple_of(who * own_requests, own_requests), own_requests)
            out[pl.ds(first, count), place, :] = total.astype(out.dtype).reshape(count, own_requests, cols)


def flip(size, bits):
    return [(i, i ^ bits) for i in range(size)]


def on_device_blocks(
    attention_output,
    output_weight,
    adapter_down_weight,
    adapter_up_weight,
    request_adapter,
    adapter_storage_row,
):
    replicas, tensors = lax.axis_size("replica"), lax.axis_size("tensor")
    steps, own_requests, feats = attention_output.shape
    cols = output_weight.shape[1] // tensors
    adapters_here, _, rank = adapter_down_weight.shape
    requests = request_adapter.shape[0]
    rows = steps * own_requests
    half = steps // 2

    def swap(value, bits):
        return lax.ppermute(value, "replica", flip(replicas, bits))

    def along(value, bits):
        return lax.ppermute(value, "tensor", flip(tensors, bits))

    passed = []

    def tie(*values):
        held = lax.optimization_barrier((*values, *passed))[: len(values)]
        return held[0] if len(values) == 1 else held

    def done(*values):
        passed[:] = values

    def wait(*values):
        passed.extend(values)

    def cost(n, width):
        return pl.CostEstimate(flops=2 * n * feats * width, bytes_accessed=2 * n * feats, transcendentals=0)

    def held_back(piece):
        return [tie(piece[0][0]), *(part for part, _, _ in piece[1:])]

    held = pltpu.VMEM((2, feats, cols), jnp.bfloat16)
    copies = pltpu.SemaphoreType.DMA((2,))

    def outer(piece, weight):
        parts = held_back(piece)
        n = sum(p.shape[0] * p.shape[1] for p in parts)
        return pl.pallas_call(
            functools.partial(outer_kernel, len(parts)),
            out_shape=jax.ShapeDtypeStruct((2, n, cols), jnp.bfloat16),
            in_specs=[VMEM] * (len(parts) + 1),
            out_specs=VMEM,
            scratch_shapes=[pltpu.VMEM((n, feats), jnp.bfloat16)],
            compiler_params=params(8),
            cost_estimate=cost(n, 2 * cols),
        )(*parts, weight)

    def inside(piece, weight, first=False):
        parts = held_back(piece)
        n = sum(p.shape[0] * p.shape[1] for p in parts)
        return pl.pallas_call(
            functools.partial(first_inner_kernel if first else inner_kernel, len(parts)),
            out_shape=[jax.ShapeDtypeStruct((n, cols), jnp.float32)] * 2 + [held] * first,
            in_specs=[VMEM] * len(parts) + [HBM if first else VMEM],
            out_specs=[VMEM] * (2 + first),
            scratch_shapes=[pltpu.VMEM((n, feats), jnp.bfloat16)] + [copies] * first,
            compiler_params=params(8),
            cost_estimate=cost(n, 2 * cols),
        )(*parts, weight)

    down = jnp.transpose(adapter_down_weight, (0, 2, 1))

    def ranked(piece, *before):
        parts = held_back(piece)
        n = sum(p.shape[0] * p.shape[1] for p in parts)
        blocks = [(bits, first) for _, bits, first in piece]
        return pl.pallas_call(
            functools.partial(rank_kernel, blocks, len(before) > 0, len(parts)),
            out_shape=jax.ShapeDtypeStruct((half * OWN_CAP, 2 * rank), jnp.float32),
            in_specs=[VMEM] * (len(parts) + 2 + len(before)),
            out_specs=VMEM,
            scratch_shapes=[pltpu.VMEM((n, feats), jnp.bfloat16)],
            compiler_params=params(10),
            cost_estimate=pl.CostEstimate(flops=0, bytes_accessed=0, transcendentals=0),
        )(*parts, down, where, *before)

    def pass_on(far, near_in):
        return (far + near_in[1].astype(jnp.float32)).astype(jnp.bfloat16)

    x0 = attention_output
    x1, x2, x4 = swap(x0, 1), swap(x0, 2), swap(x0, 4)
    weight = pltpu.with_memory_space_constraint(output_weight, pltpu.HBM)
    held_out, where = pl.pallas_call(
        functools.partial(load_kernel, replicas, steps, adapters_here),
        out_shape=[held, jax.ShapeDtypeStruct((replicas * rows, 8), jnp.int32)],
        in_specs=[HBM] * 3,
        out_specs=[VMEM] * 2,
        scratch_shapes=[
            pltpu.VMEM(request_adapter.shape, jnp.int32),
            pltpu.VMEM(adapter_storage_row.shape, jnp.int32),
            copies,
            copies,
        ],
        compiler_params=params(4),
    )(weight, *(pltpu.with_memory_space_constraint(v, pltpu.HBM) for v in (request_adapter, adapter_storage_row)))
    p0 = [(x0, 0, 0), (x1, 1, 0)]
    near0 = outer(p0, held_out)
    done(near0)
    near0_in = along(near0, 1)
    far0, own0, held_in = inside(p0, weight, True)
    done(own0)
    wait(near0_in)
    far0_out = pass_on(far0, tie(near0_in))
    far0_in = along(far0_out, 2)
    wait(far0_out)

    wait(x2, x4, near0_in)
    x2, x4 = tie(x2, x4)
    x3, x5 = swap(x2, 1), swap(x4, 1)
    x6a, x6b = swap(x2[:half], 4), swap(x4[half:], 2)
    p1 = [(x2, 2, 0), (x3, 3, 0)]
    near1 = outer(p1, held_out)
    done(near1)
    near1_in = along(near1, 1)
    wait(x5)
    p2 = [(x4, 4, 0), (x5, 5, 0)]
    near2 = outer(p2, held_out)
    done(near2)
    near2_in = along(near2, 1)
    far1, own1 = inside(p1, held_in)
    done(own1)
    far2, own2 = inside(p2, held_in)
    done(own2)

    wait(x6a, x6b)
    x6a, x6b = tie(x6a, x6b)
    x7a, x7b = swap(x6a, 1), swap(x6b, 1)
    wait(near1_in, far0_in)
    far1_out = pass_on(far1, tie(near1_in))
    far1_in = along(far1_out, 2)
    wait(far1_out, x7a, x7b)
    p3 = [(x6a, 6, 0), (x6b, 6, half), (x7a, 7, 0), (x7b, 7, half)]
    packed = ranked(p0 + p1 + p2 + p3)
    done(packed)
    packed_in = along(packed, 1)
    near3 = outer(p3, held_out)
    done(near3)
    near3_in = along(near3, 1)
    wait(near2_in, far1_in)
    far2_out = pass_on(far2, tie(near2_in))
    wait(far2_out, packed_in)
    packed = packed + tie(packed_in)
    done(packed)
    packed_in = along(packed, 2)
    far2_in = along(far2_out, 2)
    far3, own3 = inside(p3, held_in)
    done(own3)
    wait(near3_in)
    far3_out = pass_on(far3, tie(near3_in))
    far3_in = along(far3_out, 2)
    wait(far3_out)
    all_pieces = [p0, p1, p2, p3]
    arrived = [(own0, near0_in, far0_in), (own1, near1_in, far1_in), (own2, near2_in, far2_in), (own3, near3_in, far3_in)]

    def up(first, ranks, *before):
        return pl.pallas_call(
            functools.partial(up_kernel, first, len(before)),
            out_shape=jax.ShapeDtypeStruct((replicas * rows, cols), jnp.float32),
            in_specs=[VMEM] * (len(ranks) + 2 + len(before)),
            out_specs=VMEM,
            scratch_shapes=[pltpu.VMEM((replicas * rows, adapters_here * rank), jnp.bfloat16)],
            compiler_params=params(12),
        )(*ranks, adapter_up_weight, where, *before)

    wait(packed_in)
    ranks = (packed + tie(packed_in)).astype(jnp.bfloat16)[None]
    done(ranks)
    got = swap(ranks, 1)
    wait(got, far2_in)
    ranks = jnp.concatenate([ranks, tie(got)], axis=0)
    done(ranks)
    got2, got4, got6 = (swap(ranks, bits) for bits in (2, 4, 6))
    delta = up(0, [tie(ranks)])
    done(delta)
    wait(got2, got4)
    delta = up(2, [tie(got2), got4], delta)
    done(delta)
    wait(got6)
    delta = up(6, [tie(got6)], delta)

    pieces = [[(bits, first, part.shape[0]) for part, bits, first in piece] for piece in all_pieces]
    return pl.pallas_call(
        functools.partial(finish_kernel, pieces),
        out_shape=jax.ShapeDtypeStruct((steps, requests, cols), jnp.bfloat16),
        in_specs=[VMEM] * (3 * len(pieces) + 1),
        out_specs=VMEM,
        compiler_params=params(12),
    )(*[ref for piece in arrived for ref in piece], delta)


def on_device(
    attention_output,
    output_weight,
    adapter_down_weight,
    adapter_up_weight,
    request_adapter,
    adapter_storage_row,
):
    replicas = lax.axis_size("replica")
    my_index = lax.axis_index("replica")
    owner_partial = adapter_down_weight.shape[0]
    requests = request_adapter.shape[0]
    everyone = lax.all_gather(attention_output, "replica", axis=1, tiled=True)
    partial_sums = jnp.einsum(
        "sif,fc->sic", everyone, output_weight, preferred_element_type=jnp.float32
    )
    base_output = lax.psum_scatter(partial_sums, "tensor", scatter_dimension=2, tiled=True)
    adapter_ids = jnp.arange(adapter_storage_row.shape[0], dtype=jnp.int32)
    storage_row_of = jnp.sum(
        jnp.where(
            request_adapter[:, None] == adapter_ids[None, :], adapter_storage_row[None, :], 0
        ),
        axis=1,
    )
    owner_of = storage_row_of // owner_partial
    owner_table = owner_of[:, None] == jnp.arange(replicas, dtype=jnp.int32)[None, :]
    running = jnp.cumsum(owner_table.astype(jnp.int32), axis=0) - 1
    rank_in = jnp.sum(jnp.where(owner_table, running, 0), axis=1)
    owned_here = owner_of == my_index
    target = jnp.where(owned_here, rank_in, OWN_CAP)
    chosen = (
        jnp.zeros((OWN_CAP,), jnp.int32)
        .at[target]
        .set(jnp.arange(requests, dtype=jnp.int32), mode="drop")
    )
    filled = jnp.zeros((OWN_CAP,), jnp.int32).at[target].set(1, mode="drop")
    local_slot = storage_row_of[chosen] - my_index * owner_partial
    slot_pick = jnp.where(
        local_slot[:, None] == jnp.arange(owner_partial, dtype=jnp.int32)[None, :],
        filled[:, None],
        0,
    ).astype(jnp.float32)
    selected_rows = everyone[:, chosen, :]
    reduced_input = jnp.einsum(
        "ldu,hun->ldhn", selected_rows, adapter_down_weight, preferred_element_type=jnp.float32
    )
    rank_part = jnp.sum(reduced_input * slot_pick[None, :, :, None], axis=2)
    spread = jnp.where(
        owned_here[None, :, None], rank_part[:, jnp.minimum(rank_in, OWN_CAP - 1), :], 0.0
    )
    rank_full = lax.psum(spread, ("replica", "tensor"))
    rank_values = rank_full.astype(jnp.bfloat16)
    selected_up_rows = adapter_up_weight[storage_row_of]
    adapter_delta = jnp.einsum(
        "ajz,jzt->ajt", rank_values, selected_up_rows, preferred_element_type=jnp.float32
    )
    return (base_output + adapter_scale * adapter_delta).astype(jnp.bfloat16)


def solution(mesh):
    in_specs = (
        P(None, "replica", "tensor"),
        P("tensor", "replica"),
        P("replica", "tensor", None),
        P(None, None, ("replica", "tensor")),
        P(),
        P(),
    )
    out_specs = P(None, None, ("replica", "tensor"))
    blocks = mesh.shape["replica"] == 8 and mesh.shape["tensor"] == 4
    return jax.shard_map(
        on_device_blocks if blocks else on_device,
        mesh=mesh,
        in_specs=in_specs,
        out_specs=out_specs,
        check_vma=False,
    )
```

```python
import functools

import jax
import jax.numpy as jnp
from jax import lax
from jax.experimental import pallas as pl
from jax.experimental.pallas import tpu as pltpu
from jax.sharding import PartitionSpec as P

OWN_CAP = 48


adapter_scale = 0.5

MIB = 2**20
WIDE = 256
VMEM = pl.BlockSpec(memory_space=pltpu.VMEM)
HBM = pl.BlockSpec(memory_space=pltpu.HBM)
ANY = pl.BlockSpec(memory_space=pl.ANY)


def params(mib):
    return pltpu.CompilerParams(vmem_limit_bytes=mib * MIB)


def stack_rows(parts, rows_ref):
    at = 0
    for part in parts:
        steps, requests, feats = part.shape
        rows_ref[pl.ds(at, steps * requests), :] = part[...].reshape(steps * requests, feats)
        at += steps * requests


def fetch(weight, out, sems, flips):
    cols = out.shape[-1]
    mine = lax.axis_index("tensor")
    copies = []
    for slot, bits in enumerate(flips):
        chunk = pl.ds(pl.multiple_of((mine ^ bits) * cols, cols), cols)
        copies.append(pltpu.make_async_copy(weight.at[:, chunk], out.at[slot], sems.at[slot]))
    for copy in copies:
        copy.start()
    return copies


def turned(row):
    n = row.shape[1]
    same = lax.broadcasted_iota(jnp.int32, (n, n), 0) == lax.broadcasted_iota(jnp.int32, (n, n), 1)
    return jnp.sum(jnp.where(same, row, 0), axis=1, keepdims=True)


def load_kernel(replicas, steps, adapters, weight, request_in, storage_in, out, where, request, storage, sems, small):
    asked_for = pltpu.make_async_copy(request_in, request, small.at[0])
    stored_at = pltpu.make_async_copy(storage_in, storage, small.at[1])
    asked_for.start()
    stored_at.start()
    copies = fetch(weight, out, sems, (1, 3))
    me = lax.axis_index("replica")
    asked_for.wait()
    stored_at.wait()
    requests = request.shape[0]
    stored = turned(storage[...].reshape(1, storage.shape[0]))
    count = stored.shape[0]
    asked = lax.broadcasted_iota(jnp.int32, (count, requests), 0) == request[...].reshape(1, requests)
    slot_row = jnp.sum(jnp.where(asked, stored, 0), axis=0, keepdims=True)
    slot = turned(slot_row)

    def owner_of(slots):
        return sum((slots >= first * adapters).astype(jnp.int32) for first in range(1, replicas))

    owner = owner_of(slot)
    square = (requests, requests)
    earlier = lax.broadcasted_iota(jnp.int32, square, 1) < lax.broadcasted_iota(jnp.int32, square, 0)
    order = jnp.sum(jnp.where(earlier & (owner_of(slot_row) == owner), 1, 0), axis=1, keepdims=True)
    half = steps // 2
    place = owner * (steps * OWN_CAP) + order
    column = (owner ^ me) * (half * OWN_CAP) + order
    own = requests // replicas
    for replica in range(replicas):
        mine_here = slice(replica * own, (replica + 1) * own)
        for step in range(steps):
            rows = pl.ds((replica * steps + step) * own, own)
            where[rows, 0:1] = slot[mine_here]
            where[rows, 1:2] = place[mine_here] + step * OWN_CAP
            where[rows, 2:3] = column[mine_here] + (step % half) * OWN_CAP
    for copy in copies:
        copy.wait()


def outer_dots(rows, weight, near):
    cols = near.shape[-1]
    for slot in range(2):
        for at in range(0, cols, WIDE):
            where = pl.ds(at, WIDE)
            near[slot, :, where] = jnp.dot(
                rows[...], weight[slot, :, where], preferred_element_type=jnp.float32
            ).astype(near.dtype)


def outer_kernel(n, *refs):
    parts, weight, near, rows = refs[:n], *refs[n:]
    stack_rows(parts, rows)
    outer_dots(rows, weight, near)


def inner_dots(rows, weight, far, own):
    cols = own.shape[-1]
    for slot, out in enumerate((far, own)):
        for at in range(0, cols, WIDE):
            where = pl.ds(at, WIDE)
            out[:, where] = jnp.dot(rows[...], weight[slot, :, where], preferred_element_type=jnp.float32)


def first_inner_kernel(n, *refs):
    parts, whole, far, own, weight, rows, sems = refs[:n], *refs[n:]
    copies = fetch(whole, weight, sems, (2, 0))
    stack_rows(parts, rows)
    for copy in copies:
        copy.wait()
    inner_dots(rows, weight, far, own)


def inner_kernel(n, *refs):
    parts, weight, far, own, rows = refs[:n], *refs[n:]
    stack_rows(parts, rows)
    inner_dots(rows, weight, far, own)


def rank_kernel(blocks, before, n, *refs):
    parts, rest, rows = refs[:n], refs[n:-1], refs[-1]
    down, where, out = rest[0], rest[1], rest[-1]
    me = lax.axis_index("replica")
    adapters, rank, feats = down.shape
    stack_rows(parts, rows)
    total = rows.shape[0]
    whole = where.shape[0] // lax.axis_size("replica")
    here = []
    for (bits, first), part in zip(blocks, parts):
        steps, requests, _ = part.shape
        at = pl.multiple_of((me ^ bits) * whole + first * requests, requests)
        here.append(where[pl.ds(at, steps * requests), :])
    here = jnp.concatenate(here, axis=0)
    reduced = lax.dot_general(
        rows[...],
        down[...].reshape(adapters * rank, feats),
        (((1,), (1,)), ((), ())),
        preferred_element_type=jnp.float32,
    )
    local = here[:, 0:1] - me * adapters
    adapter_of = lax.broadcasted_iota(jnp.int32, (total, adapters * rank), 1) // rank
    picked = jnp.where(adapter_of == local, reduced, 0.0)
    width = adapters * rank
    while width > rank:
        width //= 2
        picked = picked[:, :width] + picked[:, width:]
    half = out.shape[0]
    packed = 2 * half
    place = here[:, 1:2] - me * packed
    chosen = (lax.broadcasted_iota(jnp.int32, (total, packed), 1) == place).astype(jnp.float32)
    packed_rank = lax.dot_general(
        chosen,
        picked,
        (((0,), (0,)), ((), ())),
        preferred_element_type=jnp.float32,
        precision=lax.Precision.HIGHEST,
    )
    value = jnp.concatenate([packed_rank[:half], packed_rank[half:]], axis=1)
    out[...] = value + rest[2][...] if before else value


def up_kernel(first, before, *refs):
    ranks, rest = refs[: -4 - before], refs[-4 - before :]
    up, where, out = rest[0], rest[1], rest[-2]
    wide = rest[-1]
    me = lax.axis_index("replica")
    total, cols = out.shape
    rank = up.shape[1]
    held = ranks[0].shape[1]
    packed_rank = jnp.concatenate([r[...].reshape(-1, r.shape[-1]) for r in ranks], axis=0)
    owners = packed_rank.shape[0] // held
    slot, column = where[:, 0:1], where[:, 2:3] - first * held
    chosen = (lax.broadcasted_iota(jnp.int32, (total, owners * held), 1) == column).astype(jnp.bfloat16)
    both = jnp.dot(chosen, packed_rank, preferred_element_type=jnp.float32)
    early_rows = total // lax.axis_size("replica") // 2
    late = (lax.broadcasted_iota(jnp.int32, (total, rank), 0) // early_rows) % 2
    rank_rows = adapter_scale * jnp.where(late == 1, both[:, rank:], both[:, :rank])
    group = wide.shape[1] // rank
    wide[...] = jnp.concatenate([rank_rows] * group, axis=1).astype(jnp.bfloat16)
    adapter_of = slot - lax.broadcasted_iota(jnp.int32, wide.shape, 1) // rank
    made = rest[2][...] if before else None
    for owner in range(owners):
        at = (me ^ (first + owner)) * group
        spread = jnp.where(adapter_of == at, wide[...], jnp.zeros_like(wide))
        weight = up[pl.ds(at, group)].reshape(group * rank, cols)
        part = jnp.dot(spread, weight, preferred_element_type=jnp.float32)
        made = part if made is None else made + part
    out[...] = made


def finish_kernel(pieces, *refs):
    out, delta = refs[-1], refs[-2]
    steps, requests, cols = out.shape
    replicas = lax.axis_size("replica")
    own_requests = requests // replicas
    me = lax.axis_index("replica")
    for i, blocks in enumerate(pieces):
        own, near, far = refs[3 * i : 3 * i + 3]
        at = 0
        for bits, first, count in blocks:
            rows = count * own_requests
            here = pl.ds(at, rows)
            at += rows
            who = me ^ bits
            total = own[here, :] + near[0, here, :].astype(jnp.float32)
            total += far[here, :].astype(jnp.float32)
            start = pl.multiple_of((who * steps + first) * own_requests, own_requests)
            total += delta[pl.ds(start, rows), :]
            place = pl.ds(pl.multiple_of(who * own_requests, own_requests), own_requests)
            out[pl.ds(first, count), place, :] = total.astype(out.dtype).reshape(count, own_requests, cols)


def flip(size, bits):
    return [(i, i ^ bits) for i in range(size)]


def on_device_blocks(
    attention_output,
    output_weight,
    adapter_down_weight,
    adapter_up_weight,
    request_adapter,
    adapter_storage_row,
):
    replicas, tensors = lax.axis_size("replica"), lax.axis_size("tensor")
    steps, own_requests, feats = attention_output.shape
    cols = output_weight.shape[1] // tensors
    adapters_here, _, rank = adapter_down_weight.shape
    requests = request_adapter.shape[0]
    rows = steps * own_requests
    half = steps // 2

    def swap(value, bits):
        return lax.ppermute(value, "replica", flip(replicas, bits))

    def along(value, bits):
        return lax.ppermute(value, "tensor", flip(tensors, bits))

    passed = []

    def tie(*values):
        held = lax.optimization_barrier((*values, *passed))[: len(values)]
        return held[0] if len(values) == 1 else held

    def done(*values):
        passed[:] = values

    def wait(*values):
        passed.extend(values)

    def cost(n, width):
        return pl.CostEstimate(flops=2 * n * feats * width, bytes_accessed=2 * n * feats, transcendentals=0)

    def held_back(piece):
        return [tie(piece[0][0]), *(part for part, _, _ in piece[1:])]

    held = pltpu.VMEM((2, feats, cols), jnp.bfloat16)
    copies = pltpu.SemaphoreType.DMA((2,))

    def outer(piece, weight):
        parts = held_back(piece)
        n = sum(p.shape[0] * p.shape[1] for p in parts)
        return pl.pallas_call(
            functools.partial(outer_kernel, len(parts)),
            out_shape=jax.ShapeDtypeStruct((2, n, cols), jnp.bfloat16),
            in_specs=[VMEM] * (len(parts) + 1),
            out_specs=VMEM,
            scratch_shapes=[pltpu.VMEM((n, feats), jnp.bfloat16)],
            compiler_params=params(8),
            cost_estimate=cost(n, 2 * cols),
        )(*parts, weight)

    def inside(piece, weight, first=False):
        parts = held_back(piece)
        n = sum(p.shape[0] * p.shape[1] for p in parts)
        return pl.pallas_call(
            functools.partial(first_inner_kernel if first else inner_kernel, len(parts)),
            out_shape=[jax.ShapeDtypeStruct((n, cols), jnp.float32)] * 2 + [held] * first,
            in_specs=[VMEM] * len(parts) + [HBM if first else VMEM],
            out_specs=[VMEM] * (2 + first),
            scratch_shapes=[pltpu.VMEM((n, feats), jnp.bfloat16)] + [copies] * first,
            compiler_params=params(8),
            cost_estimate=cost(n, 2 * cols),
        )(*parts, weight)

    down = jnp.transpose(adapter_down_weight, (0, 2, 1))

    def ranked(piece, *before):
        parts = held_back(piece)
        n = sum(p.shape[0] * p.shape[1] for p in parts)
        blocks = [(bits, first) for _, bits, first in piece]
        return pl.pallas_call(
            functools.partial(rank_kernel, blocks, len(before) > 0, len(parts)),
            out_shape=jax.ShapeDtypeStruct((half * OWN_CAP, 2 * rank), jnp.float32),
            in_specs=[VMEM] * (len(parts) + 2 + len(before)),
            out_specs=VMEM,
            scratch_shapes=[pltpu.VMEM((n, feats), jnp.bfloat16)],
            compiler_params=params(10),
            cost_estimate=pl.CostEstimate(flops=0, bytes_accessed=0, transcendentals=0),
        )(*parts, down, where, *before)

    def pass_on(far, near_in):
        return (far + near_in[1].astype(jnp.float32)).astype(jnp.bfloat16)

    x0 = attention_output
    x1, x2, x4 = swap(x0, 1), swap(x0, 2), swap(x0, 4)
    weight = pltpu.with_memory_space_constraint(output_weight, pltpu.HBM)
    held_out, where = pl.pallas_call(
        functools.partial(load_kernel, replicas, steps, adapters_here),
        out_shape=[held, jax.ShapeDtypeStruct((replicas * rows, 8), jnp.int32)],
        in_specs=[HBM] * 3,
        out_specs=[VMEM] * 2,
        scratch_shapes=[
            pltpu.VMEM(request_adapter.shape, jnp.int32),
            pltpu.VMEM(adapter_storage_row.shape, jnp.int32),
            copies,
            copies,
        ],
        compiler_params=params(4),
    )(weight, *(pltpu.with_memory_space_constraint(v, pltpu.HBM) for v in (request_adapter, adapter_storage_row)))
    p0 = [(x0, 0, 0), (x1, 1, 0)]
    near0 = outer(p0, held_out)
    done(near0)
    near0_in = along(near0, 1)
    far0, own0, held_in = inside(p0, weight, True)
    done(own0)
    wait(near0_in)
    far0_out = pass_on(far0, tie(near0_in))
    far0_in = along(far0_out, 2)
    wait(far0_out)

    wait(x2, x4, near0_in)
    x2, x4 = tie(x2, x4)
    x3, x5 = swap(x2, 1), swap(x4, 1)
    x6a, x6b = swap(x2[:half], 4), swap(x4[half:], 2)
    p1 = [(x2, 2, 0), (x3, 3, 0)]
    near1 = outer(p1, held_out)
    done(near1)
    near1_in = along(near1, 1)
    wait(x5)
    p2 = [(x4, 4, 0), (x5, 5, 0)]
    near2 = outer(p2, held_out)
    done(near2)
    near2_in = along(near2, 1)
    far1, own1 = inside(p1, held_in)
    done(own1)
    far2, own2 = inside(p2, held_in)
    done(own2)

    wait(x6a, x6b)
    x6a, x6b = tie(x6a, x6b)
    x7a, x7b = swap(x6a, 1), swap(x6b, 1)
    packed = ranked(p0 + p1 + p2)
    done(packed)
    wait(near1_in, far0_in)
    far1_out = pass_on(far1, tie(near1_in))
    far1_in = along(far1_out, 2)
    wait(far1_out, x7a, x7b)
    p3 = [(x6a, 6, 0), (x6b, 6, half), (x7a, 7, 0), (x7b, 7, half)]
    packed = ranked(p3, packed)
    done(packed)
    packed_in = along(packed, 1)
    near3 = outer(p3, held_out)
    done(near3)
    near3_in = along(near3, 1)
    wait(near2_in, far1_in)
    far2_out = pass_on(far2, tie(near2_in))
    wait(far2_out, packed_in)
    packed = packed + tie(packed_in)
    done(packed)
    packed_in = along(packed, 2)
    far2_in = along(far2_out, 2)
    far3, own3 = inside(p3, held_in)
    done(own3)
    wait(near3_in)
    far3_out = pass_on(far3, tie(near3_in))
    far3_in = along(far3_out, 2)
    wait(far3_out)

    def up(first, ranks, *before):
        return pl.pallas_call(
            functools.partial(up_kernel, first, len(before)),
            out_shape=jax.ShapeDtypeStruct((replicas * rows, cols), jnp.float32),
            in_specs=[VMEM] * (len(ranks) + 2 + len(before)),
            out_specs=VMEM,
            scratch_shapes=[pltpu.VMEM((replicas * rows, adapters_here * rank), jnp.bfloat16)],
            compiler_params=params(12),
        )(*ranks, adapter_up_weight, where, *before)

    wait(packed_in)
    ranks = (packed + tie(packed_in)).astype(jnp.bfloat16)[None]
    done(ranks)
    got = swap(ranks, 1)
    wait(got, far2_in)
    ranks = jnp.concatenate([ranks, tie(got)], axis=0)
    done(ranks)
    got2, got4, got6 = (swap(ranks, bits) for bits in (2, 4, 6))
    delta = up(0, [tie(ranks)])
    done(delta)
    wait(got2, got4)
    delta = up(2, [tie(got2), got4], delta)
    done(delta)
    wait(got6)
    delta = up(6, [tie(got6)], delta)

    all_pieces = [p0, p1, p2, p3]
    arrived = [(own0, near0_in, far0_in), (own1, near1_in, far1_in), (own2, near2_in, far2_in), (own3, near3_in, far3_in)]
    pieces = [[(bits, first, part.shape[0]) for part, bits, first in piece] for piece in all_pieces]
    return pl.pallas_call(
        functools.partial(finish_kernel, pieces),
        out_shape=jax.ShapeDtypeStruct((steps, requests, cols), jnp.bfloat16),
        in_specs=[VMEM] * (3 * len(pieces) + 1),
        out_specs=VMEM,
        compiler_params=params(12),
    )(*[ref for piece in arrived for ref in piece], delta)


def on_device(
    attention_output,
    output_weight,
    adapter_down_weight,
    adapter_up_weight,
    request_adapter,
    adapter_storage_row,
):
    replicas = lax.axis_size("replica")
    my_index = lax.axis_index("replica")
    owner_partial = adapter_down_weight.shape[0]
    requests = request_adapter.shape[0]
    everyone = lax.all_gather(attention_output, "replica", axis=1, tiled=True)
    partial_sums = jnp.einsum(
        "sif,fc->sic", everyone, output_weight, preferred_element_type=jnp.float32
    )
    base_output = lax.psum_scatter(partial_sums, "tensor", scatter_dimension=2, tiled=True)
    adapter_ids = jnp.arange(adapter_storage_row.shape[0], dtype=jnp.int32)
    storage_row_of = jnp.sum(
        jnp.where(
            request_adapter[:, None] == adapter_ids[None, :], adapter_storage_row[None, :], 0
        ),
        axis=1,
    )
    owner_of = storage_row_of // owner_partial
    owner_table = owner_of[:, None] == jnp.arange(replicas, dtype=jnp.int32)[None, :]
    running = jnp.cumsum(owner_table.astype(jnp.int32), axis=0) - 1
    rank_in = jnp.sum(jnp.where(owner_table, running, 0), axis=1)
    owned_here = owner_of == my_index
    target = jnp.where(owned_here, rank_in, OWN_CAP)
    chosen = (
        jnp.zeros((OWN_CAP,), jnp.int32)
        .at[target]
        .set(jnp.arange(requests, dtype=jnp.int32), mode="drop")
    )
    filled = jnp.zeros((OWN_CAP,), jnp.int32).at[target].set(1, mode="drop")
    local_slot = storage_row_of[chosen] - my_index * owner_partial
    slot_pick = jnp.where(
        local_slot[:, None] == jnp.arange(owner_partial, dtype=jnp.int32)[None, :],
        filled[:, None],
        0,
    ).astype(jnp.float32)
    selected_rows = everyone[:, chosen, :]
    reduced_input = jnp.einsum(
        "ldu,hun->ldhn", selected_rows, adapter_down_weight, preferred_element_type=jnp.float32
    )
    rank_part = jnp.sum(reduced_input * slot_pick[None, :, :, None], axis=2)
    spread = jnp.where(
        owned_here[None, :, None], rank_part[:, jnp.minimum(rank_in, OWN_CAP - 1), :], 0.0
    )
    rank_full = lax.psum(spread, ("replica", "tensor"))
    rank_values = rank_full.astype(jnp.bfloat16)
    selected_up_rows = adapter_up_weight[storage_row_of]
    adapter_delta = jnp.einsum(
        "ajz,jzt->ajt", rank_values, selected_up_rows, preferred_element_type=jnp.float32
    )
    return (base_output + adapter_scale * adapter_delta).astype(jnp.bfloat16)


def solution(mesh):
    in_specs = (
        P(None, "replica", "tensor"),
        P("tensor", "replica"),
        P("replica", "tensor", None),
        P(None, None, ("replica", "tensor")),
        P(),
        P(),
    )
    out_specs = P(None, None, ("replica", "tensor"))
    blocks = mesh.shape["replica"] == 8 and mesh.shape["tensor"] == 4
    return jax.shard_map(
        on_device_blocks if blocks else on_device,
        mesh=mesh,
        in_specs=in_specs,
        out_specs=out_specs,
        check_vma=False,
    )
```

```python
import functools

import jax
import jax.numpy as jnp
from jax import lax
from jax.experimental import pallas as pl
from jax.experimental.pallas import tpu as pltpu
from jax.sharding import PartitionSpec as P

OWN_CAP = 48


adapter_scale = 0.5

MIB = 2**20
WIDE = 256
VMEM = pl.BlockSpec(memory_space=pltpu.VMEM)
HBM = pl.BlockSpec(memory_space=pltpu.HBM)
ANY = pl.BlockSpec(memory_space=pl.ANY)


def params(mib):
    return pltpu.CompilerParams(vmem_limit_bytes=mib * MIB)


def stack_rows(parts, rows_ref):
    at = 0
    for part in parts:
        steps, requests, feats = part.shape
        rows_ref[pl.ds(at, steps * requests), :] = part[...].reshape(steps * requests, feats)
        at += steps * requests


def fetch(weight, out, sems, flips):
    cols = out.shape[-1]
    mine = lax.axis_index("tensor")
    copies = []
    for slot, bits in enumerate(flips):
        chunk = pl.ds(pl.multiple_of((mine ^ bits) * cols, cols), cols)
        copies.append(pltpu.make_async_copy(weight.at[:, chunk], out.at[slot], sems.at[slot]))
    for copy in copies:
        copy.start()
    return copies


def turned(row):
    n = row.shape[1]
    same = lax.broadcasted_iota(jnp.int32, (n, n), 0) == lax.broadcasted_iota(jnp.int32, (n, n), 1)
    return jnp.sum(jnp.where(same, row, 0), axis=1, keepdims=True)


def load_kernel(replicas, steps, adapters, weight, request_in, storage_in, out, where, request, storage, sems, small):
    asked_for = pltpu.make_async_copy(request_in, request, small.at[0])
    stored_at = pltpu.make_async_copy(storage_in, storage, small.at[1])
    asked_for.start()
    stored_at.start()
    copies = fetch(weight, out, sems, (1, 3))
    me = lax.axis_index("replica")
    asked_for.wait()
    stored_at.wait()
    requests = request.shape[0]
    stored = turned(storage[...].reshape(1, storage.shape[0]))
    count = stored.shape[0]
    asked = lax.broadcasted_iota(jnp.int32, (count, requests), 0) == request[...].reshape(1, requests)
    slot_row = jnp.sum(jnp.where(asked, stored, 0), axis=0, keepdims=True)
    slot = turned(slot_row)

    def owner_of(slots):
        return sum((slots >= first * adapters).astype(jnp.int32) for first in range(1, replicas))

    owner = owner_of(slot)
    square = (requests, requests)
    earlier = lax.broadcasted_iota(jnp.int32, square, 1) < lax.broadcasted_iota(jnp.int32, square, 0)
    order = jnp.sum(jnp.where(earlier & (owner_of(slot_row) == owner), 1, 0), axis=1, keepdims=True)
    half = steps // 2
    place = owner * (steps * OWN_CAP) + order
    column = (owner ^ me) * (half * OWN_CAP) + order
    own = requests // replicas
    for replica in range(replicas):
        mine_here = slice(replica * own, (replica + 1) * own)
        for step in range(steps):
            rows = pl.ds((replica * steps + step) * own, own)
            where[rows, 0:1] = slot[mine_here]
            where[rows, 1:2] = place[mine_here] + step * OWN_CAP
            where[rows, 2:3] = column[mine_here] + (step % half) * OWN_CAP
    for copy in copies:
        copy.wait()


def outer_dots(rows, weight, near):
    cols = near.shape[-1]
    for slot in range(2):
        for at in range(0, cols, WIDE):
            where = pl.ds(at, WIDE)
            near[slot, :, where] = jnp.dot(
                rows[...], weight[slot, :, where], preferred_element_type=jnp.float32
            ).astype(near.dtype)


def outer_kernel(n, *refs):
    parts, weight, near, rows = refs[:n], *refs[n:]
    stack_rows(parts, rows)
    outer_dots(rows, weight, near)


def inner_dots(rows, weight, far, own):
    cols = own.shape[-1]
    for slot, out in enumerate((far, own)):
        for at in range(0, cols, WIDE):
            where = pl.ds(at, WIDE)
            out[:, where] = jnp.dot(rows[...], weight[slot, :, where], preferred_element_type=jnp.float32)


def first_inner_kernel(n, *refs):
    parts, whole, down, far, own, weight, turned_down, rows, sems = refs[:n], *refs[n:]
    copies = fetch(whole, weight, sems, (2, 0))
    stack_rows(parts, rows)
    adapters, rank, feats = down.shape
    pair = 128 // rank
    for first in range(0, adapters, pair):
        for at in range(0, feats, WIDE):
            some = pl.ds(at, WIDE)
            block = down[pl.ds(first, pair), :, some].reshape(pair * rank, WIDE)
            turned_down[some, pl.ds(first * rank, pair * rank)] = block.T
    for copy in copies:
        copy.wait()
    inner_dots(rows, weight, far, own)


def inner_kernel(n, *refs):
    parts, weight, far, own, rows = refs[:n], *refs[n:]
    stack_rows(parts, rows)
    inner_dots(rows, weight, far, own)


def rank_kernel(blocks, before, n, *refs):
    parts, rest, rows = refs[:n], refs[n:-1], refs[-1]
    down, where, out = rest[0], rest[1], rest[-1]
    me = lax.axis_index("replica")
    rank = out.shape[1] // 2
    adapters = down.shape[1] // rank
    stack_rows(parts, rows)
    total = rows.shape[0]
    whole = where.shape[0] // lax.axis_size("replica")
    here = []
    for (bits, first), part in zip(blocks, parts):
        steps, requests, _ = part.shape
        at = pl.multiple_of((me ^ bits) * whole + first * requests, requests)
        here.append(where[pl.ds(at, steps * requests), :])
    here = jnp.concatenate(here, axis=0)
    reduced = jnp.dot(rows[...], down[...], preferred_element_type=jnp.float32)
    local = here[:, 0:1] - me * adapters
    adapter_of = lax.broadcasted_iota(jnp.int32, (total, adapters * rank), 1) // rank
    picked = jnp.where(adapter_of == local, reduced, 0.0)
    width = adapters * rank
    while width > rank:
        width //= 2
        picked = picked[:, :width] + picked[:, width:]
    half = out.shape[0]
    packed = 2 * half
    place = here[:, 1:2] - me * packed
    chosen = (lax.broadcasted_iota(jnp.int32, (total, packed), 1) == place).astype(jnp.float32)
    packed_rank = lax.dot_general(
        chosen,
        picked,
        (((0,), (0,)), ((), ())),
        preferred_element_type=jnp.float32,
        precision=lax.Precision.HIGHEST,
    )
    value = jnp.concatenate([packed_rank[:half], packed_rank[half:]], axis=1)
    out[...] = value + rest[2][...] if before else value


def up_kernel(first, before, *refs):
    ranks, rest = refs[: -4 - before], refs[-4 - before :]
    up, where, out = rest[0], rest[1], rest[-2]
    wide = rest[-1]
    me = lax.axis_index("replica")
    total, cols = out.shape
    rank = up.shape[1]
    held = ranks[0].shape[1]
    packed_rank = jnp.concatenate([r[...].reshape(-1, r.shape[-1]) for r in ranks], axis=0)
    owners = packed_rank.shape[0] // held
    slot, column = where[:, 0:1], where[:, 2:3] - first * held
    chosen = (lax.broadcasted_iota(jnp.int32, (total, owners * held), 1) == column).astype(jnp.bfloat16)
    both = jnp.dot(chosen, packed_rank, preferred_element_type=jnp.float32)
    early_rows = total // lax.axis_size("replica") // 2
    late = (lax.broadcasted_iota(jnp.int32, (total, rank), 0) // early_rows) % 2
    rank_rows = adapter_scale * jnp.where(late == 1, both[:, rank:], both[:, :rank])
    group = wide.shape[1] // rank
    wide[...] = jnp.concatenate([rank_rows] * group, axis=1).astype(jnp.bfloat16)
    adapter_of = slot - lax.broadcasted_iota(jnp.int32, wide.shape, 1) // rank
    made = rest[2][...] if before else None
    for owner in range(owners):
        at = (me ^ (first + owner)) * group
        spread = jnp.where(adapter_of == at, wide[...], jnp.zeros_like(wide))
        weight = up[pl.ds(at, group)].reshape(group * rank, cols)
        part = jnp.dot(spread, weight, preferred_element_type=jnp.float32)
        made = part if made is None else made + part
    out[...] = made


def finish_kernel(pieces, *refs):
    out, delta = refs[-1], refs[-2]
    steps, requests, cols = out.shape
    replicas = lax.axis_size("replica")
    own_requests = requests // replicas
    me = lax.axis_index("replica")
    for i, blocks in enumerate(pieces):
        own, near, far = refs[3 * i : 3 * i + 3]
        at = 0
        for bits, first, count in blocks:
            rows = count * own_requests
            here = pl.ds(at, rows)
            at += rows
            who = me ^ bits
            total = own[here, :] + near[0, here, :].astype(jnp.float32)
            total += far[here, :].astype(jnp.float32)
            start = pl.multiple_of((who * steps + first) * own_requests, own_requests)
            total += delta[pl.ds(start, rows), :]
            place = pl.ds(pl.multiple_of(who * own_requests, own_requests), own_requests)
            out[pl.ds(first, count), place, :] = total.astype(out.dtype).reshape(count, own_requests, cols)


def flip(size, bits):
    return [(i, i ^ bits) for i in range(size)]


def on_device_blocks(
    attention_output,
    output_weight,
    adapter_down_weight,
    adapter_up_weight,
    request_adapter,
    adapter_storage_row,
):
    replicas, tensors = lax.axis_size("replica"), lax.axis_size("tensor")
    steps, own_requests, feats = attention_output.shape
    cols = output_weight.shape[1] // tensors
    adapters_here, _, rank = adapter_down_weight.shape
    requests = request_adapter.shape[0]
    rows = steps * own_requests
    half = steps // 2

    def swap(value, bits):
        return lax.ppermute(value, "replica", flip(replicas, bits))

    def along(value, bits):
        return lax.ppermute(value, "tensor", flip(tensors, bits))

    passed = []

    def tie(*values):
        held = lax.optimization_barrier((*values, *passed))[: len(values)]
        return held[0] if len(values) == 1 else held

    def done(*values):
        passed[:] = values

    def wait(*values):
        passed.extend(values)

    def cost(n, width):
        return pl.CostEstimate(flops=2 * n * feats * width, bytes_accessed=2 * n * feats, transcendentals=0)

    def held_back(piece):
        return [tie(piece[0][0]), *(part for part, _, _ in piece[1:])]

    held = pltpu.VMEM((2, feats, cols), jnp.bfloat16)
    copies = pltpu.SemaphoreType.DMA((2,))

    def outer(piece, weight):
        parts = held_back(piece)
        n = sum(p.shape[0] * p.shape[1] for p in parts)
        return pl.pallas_call(
            functools.partial(outer_kernel, len(parts)),
            out_shape=jax.ShapeDtypeStruct((2, n, cols), jnp.bfloat16),
            in_specs=[VMEM] * (len(parts) + 1),
            out_specs=VMEM,
            scratch_shapes=[pltpu.VMEM((n, feats), jnp.bfloat16)],
            compiler_params=params(8),
            cost_estimate=cost(n, 2 * cols),
        )(*parts, weight)

    def inside(piece, weight, *extra):
        parts = held_back(piece)
        n = sum(p.shape[0] * p.shape[1] for p in parts)
        first = len(extra) > 0
        return pl.pallas_call(
            functools.partial(first_inner_kernel if first else inner_kernel, len(parts)),
            out_shape=[jax.ShapeDtypeStruct((n, cols), jnp.float32)] * 2
            + [held, pltpu.VMEM((feats, adapters_here * rank), jnp.bfloat16)] * first,
            in_specs=[VMEM] * len(parts) + [HBM if first else VMEM] + [VMEM] * first,
            out_specs=[VMEM] * (2 + 2 * first),
            scratch_shapes=[pltpu.VMEM((n, feats), jnp.bfloat16)] + [copies] * first,
            compiler_params=params(8),
            cost_estimate=cost(n, 2 * cols),
        )(*parts, weight, *extra)

    down = jnp.transpose(adapter_down_weight, (0, 2, 1))

    def ranked(piece, *before):
        parts = held_back(piece)
        n = sum(p.shape[0] * p.shape[1] for p in parts)
        blocks = [(bits, first) for _, bits, first in piece]
        return pl.pallas_call(
            functools.partial(rank_kernel, blocks, len(before) > 0, len(parts)),
            out_shape=jax.ShapeDtypeStruct((half * OWN_CAP, 2 * rank), jnp.float32),
            in_specs=[VMEM] * (len(parts) + 2 + len(before)),
            out_specs=VMEM,
            scratch_shapes=[pltpu.VMEM((n, feats), jnp.bfloat16)],
            compiler_params=params(10),
            cost_estimate=pl.CostEstimate(flops=0, bytes_accessed=0, transcendentals=0),
        )(*parts, turned_down, where, *before)

    def pass_on(far, near_in):
        return (far + near_in[1].astype(jnp.float32)).astype(jnp.bfloat16)

    x0 = attention_output
    x1, x2, x4 = swap(x0, 1), swap(x0, 2), swap(x0, 4)
    weight = pltpu.with_memory_space_constraint(output_weight, pltpu.HBM)
    held_out, where = pl.pallas_call(
        functools.partial(load_kernel, replicas, steps, adapters_here),
        out_shape=[held, jax.ShapeDtypeStruct((replicas * rows, 8), jnp.int32)],
        in_specs=[HBM] * 3,
        out_specs=[VMEM] * 2,
        scratch_shapes=[
            pltpu.VMEM(request_adapter.shape, jnp.int32),
            pltpu.VMEM(adapter_storage_row.shape, jnp.int32),
            copies,
            copies,
        ],
        compiler_params=params(4),
    )(weight, *(pltpu.with_memory_space_constraint(v, pltpu.HBM) for v in (request_adapter, adapter_storage_row)))
    p0 = [(x0, 0, 0), (x1, 1, 0)]
    near0 = outer(p0, held_out)
    done(near0)
    near0_in = along(near0, 1)
    far0, own0, held_in, turned_down = inside(p0, weight, down)
    done(own0)
    wait(near0_in)
    far0_out = pass_on(far0, tie(near0_in))
    far0_in = along(far0_out, 2)
    wait(far0_out)

    wait(x2, x4, near0_in)
    x2, x4 = tie(x2, x4)
    x3, x5 = swap(x2, 1), swap(x4, 1)
    x6a, x6b = swap(x2[:half], 4), swap(x4[half:], 2)
    p1 = [(x2, 2, 0), (x3, 3, 0)]
    near1 = outer(p1, held_out)
    done(near1)
    near1_in = along(near1, 1)
    wait(x5)
    p2 = [(x4, 4, 0), (x5, 5, 0)]
    near2 = outer(p2, held_out)
    done(near2)
    near2_in = along(near2, 1)
    far1, own1 = inside(p1, held_in)
    done(own1)
    far2, own2 = inside(p2, held_in)
    done(own2)

    wait(x6a, x6b)
    x6a, x6b = tie(x6a, x6b)
    x7a, x7b = swap(x6a, 1), swap(x6b, 1)
    packed = ranked(p0 + p1 + p2)
    done(packed)
    wait(near1_in, far0_in)
    far1_out = pass_on(far1, tie(near1_in))
    far1_in = along(far1_out, 2)
    wait(far1_out, x7a, x7b)
    p3 = [(x6a, 6, 0), (x6b, 6, half), (x7a, 7, 0), (x7b, 7, half)]
    packed = ranked(p3, packed)
    done(packed)
    packed_in = along(packed, 1)
    near3 = outer(p3, held_out)
    done(near3)
    near3_in = along(near3, 1)
    wait(packed_in, far1_in)
    packed = packed + tie(packed_in)
    done(packed)
    packed_in = along(packed, 2)
    wait(near2_in)
    far2_out = pass_on(far2, tie(near2_in))
    far2_in = along(far2_out, 2)
    wait(far2_out)
    far3, own3 = inside(p3, held_in)
    done(own3)
    wait(near3_in)
    far3_out = pass_on(far3, tie(near3_in))
    far3_in = along(far3_out, 2)
    wait(far3_out)

    def up(first, ranks, *before):
        return pl.pallas_call(
            functools.partial(up_kernel, first, len(before)),
            out_shape=jax.ShapeDtypeStruct((replicas * rows, cols), jnp.float32),
            in_specs=[VMEM] * (len(ranks) + 2 + len(before)),
            out_specs=VMEM,
            scratch_shapes=[pltpu.VMEM((replicas * rows, adapters_here * rank), jnp.bfloat16)],
            compiler_params=params(12),
        )(*ranks, adapter_up_weight, where, *before)

    wait(packed_in)
    ranks = (packed + tie(packed_in)).astype(jnp.bfloat16)[None]
    done(ranks)
    got = swap(ranks, 1)
    wait(got, far2_in)
    ranks = jnp.concatenate([ranks, tie(got)], axis=0)
    done(ranks)
    got2, got4, got6 = (swap(ranks, bits) for bits in (2, 4, 6))
    delta = up(0, [tie(ranks)])
    done(delta)
    wait(got2, got4)
    delta = up(2, [tie(got2), got4], delta)
    done(delta)
    wait(got6)
    delta = up(6, [tie(got6)], delta)

    all_pieces = [p0, p1, p2, p3]
    arrived = [(own0, near0_in, far0_in), (own1, near1_in, far1_in), (own2, near2_in, far2_in), (own3, near3_in, far3_in)]
    pieces = [[(bits, first, part.shape[0]) for part, bits, first in piece] for piece in all_pieces]
    return pl.pallas_call(
        functools.partial(finish_kernel, pieces),
        out_shape=jax.ShapeDtypeStruct((steps, requests, cols), jnp.bfloat16),
        in_specs=[VMEM] * (3 * len(pieces) + 1),
        out_specs=VMEM,
        compiler_params=params(12),
    )(*[ref for piece in arrived for ref in piece], delta)


def on_device(
    attention_output,
    output_weight,
    adapter_down_weight,
    adapter_up_weight,
    request_adapter,
    adapter_storage_row,
):
    replicas = lax.axis_size("replica")
    my_index = lax.axis_index("replica")
    owner_partial = adapter_down_weight.shape[0]
    requests = request_adapter.shape[0]
    everyone = lax.all_gather(attention_output, "replica", axis=1, tiled=True)
    partial_sums = jnp.einsum(
        "sif,fc->sic", everyone, output_weight, preferred_element_type=jnp.float32
    )
    base_output = lax.psum_scatter(partial_sums, "tensor", scatter_dimension=2, tiled=True)
    adapter_ids = jnp.arange(adapter_storage_row.shape[0], dtype=jnp.int32)
    storage_row_of = jnp.sum(
        jnp.where(
            request_adapter[:, None] == adapter_ids[None, :], adapter_storage_row[None, :], 0
        ),
        axis=1,
    )
    owner_of = storage_row_of // owner_partial
    owner_table = owner_of[:, None] == jnp.arange(replicas, dtype=jnp.int32)[None, :]
    running = jnp.cumsum(owner_table.astype(jnp.int32), axis=0) - 1
    rank_in = jnp.sum(jnp.where(owner_table, running, 0), axis=1)
    owned_here = owner_of == my_index
    target = jnp.where(owned_here, rank_in, OWN_CAP)
    chosen = (
        jnp.zeros((OWN_CAP,), jnp.int32)
        .at[target]
        .set(jnp.arange(requests, dtype=jnp.int32), mode="drop")
    )
    filled = jnp.zeros((OWN_CAP,), jnp.int32).at[target].set(1, mode="drop")
    local_slot = storage_row_of[chosen] - my_index * owner_partial
    slot_pick = jnp.where(
        local_slot[:, None] == jnp.arange(owner_partial, dtype=jnp.int32)[None, :],
        filled[:, None],
        0,
    ).astype(jnp.float32)
    selected_rows = everyone[:, chosen, :]
    reduced_input = jnp.einsum(
        "ldu,hun->ldhn", selected_rows, adapter_down_weight, preferred_element_type=jnp.float32
    )
    rank_part = jnp.sum(reduced_input * slot_pick[None, :, :, None], axis=2)
    spread = jnp.where(
        owned_here[None, :, None], rank_part[:, jnp.minimum(rank_in, OWN_CAP - 1), :], 0.0
    )
    rank_full = lax.psum(spread, ("replica", "tensor"))
    rank_values = rank_full.astype(jnp.bfloat16)
    selected_up_rows = adapter_up_weight[storage_row_of]
    adapter_delta = jnp.einsum(
        "ajz,jzt->ajt", rank_values, selected_up_rows, preferred_element_type=jnp.float32
    )
    return (base_output + adapter_scale * adapter_delta).astype(jnp.bfloat16)


def solution(mesh):
    in_specs = (
        P(None, "replica", "tensor"),
        P("tensor", "replica"),
        P("replica", "tensor", None),
        P(None, None, ("replica", "tensor")),
        P(),
        P(),
    )
    out_specs = P(None, None, ("replica", "tensor"))
    blocks = mesh.shape["replica"] == 8 and mesh.shape["tensor"] == 4
    return jax.shard_map(
        on_device_blocks if blocks else on_device,
        mesh=mesh,
        in_specs=in_specs,
        out_specs=out_specs,
        check_vma=False,
    )
```
